32 devices in a mesh: grp: 2 (over y), ctx: 1, mdl: 8 (over z, x), dp: 2 (over core).
Axes of the slice: x: 2, y: 2, z: 4, core: 2. Of those that a mesh axis runs over, the one named last changes fastest.
Arguments:
- layer_input: bfloat16 [4, 1024, 2560], P(('grp', 'dp'), 'ctx', 'mdl'), parts along dimension 0, may hold values from -6 to 6
- read_weight: bfloat16 [2560, 128], P('mdl'), may hold values from -0.125 to 0.125
- head_inputs: bfloat16 [4, 1024, 5120], P(('grp', 'dp'), 'ctx', 'mdl'), parts along dimension 0, may hold values from -6 to 6
- write_vectors: bfloat16 [4, 1024, 128], P(('grp', 'dp'), 'ctx'), parts along dimension 0, may hold values from -0.0034179688 to 0.0034179688
- log_decay: float32 [4, 80, 1024], P(('grp', 'dp'), 'mdl', 'ctx'), parts along dimension 0, may hold values from -1 to 0
- segment_ids: int32 [4, 1024], P(('grp', 'dp'), 'ctx'), parts along dimension 0, may hold values from 0 to 3, never falling along the last dimension, each value on 1 to 512 neighbouring positions
- out_grad: bfloat16 [4, 1024, 5120], P(('grp', 'dp'), 'ctx', 'mdl'), parts along dimension 0, may hold values from -0.0029296875 to 0.0029296875
Outputs:
- head_outputs: bfloat16 [4, 1024, 5120], P(('grp', 'dp'), 'ctx', 'mdl'), parts along dimension 0
- read_grad: float32 [256, 2560], P(('grp', 'ctx', 'dp'), 'mdl'), parts along dimension 0
The draws below stay inside these ranges and needn't reach their ends.
There are 2 independent parts, one for each index of `grp`. The reference program is written for one: setup_inputs(seed, part) draws one part's arguments, and reference() takes and returns one part's arrays. A program takes and returns all parts, laid end to end along the dimension named above; an argument that names none is the same for every part. Nothing has to cross between parts.
Inputs may be any that keep to these rules, and one draw needn't show every extreme that they name: `segment_ids`: segment numbers never fall along a trace; each segment is a run of at most 512 positions.
All inputs are finite; a program needn't handle non-finite values.
Results may differ from the reference program's by a relative error of at most 0.015.
Values may be sent and summed in bfloat16 or wider, within the bound.
A program may use at most 64 MiB of HBM per device.

```python
import math
import jax
import jax.numpy as jnp
import numpy as np
from jax import lax

D = 2560
N = 128
HEADS = 80
P_SIZE = 64
BLOCK_LEN = 512
L_DEV = 1024
TRACES = 2
SEQ = 1024
HP = 5120
N_MDL = 8


def draw_log_decay(key, part):
    streams = jax.random.split(key, 7)
    fast_share = 0.5
    selector = jax.random.uniform(streams[0], (TRACES, HEADS, 1, 1))
    fast_rate = jnp.exp(jax.random.uniform(streams[1], (TRACES, HEADS, 1, 1), minval=math.log(1.0 / 50.0), maxval=math.log(1.0 / 30.0)))
    gradual_decay_speed = jnp.exp(jax.random.uniform(streams[2], (TRACES, HEADS, 1, 1), minval=math.log(0.05), maxval=math.log(0.2))) / SEQ
    base_rate = jnp.where(selector < fast_share, fast_rate, gradual_decay_speed)
    shard_count = SEQ // L_DEV
    shard_factor = jnp.exp(jax.random.uniform(streams[3], (TRACES, HEADS, shard_count, 1), minval=math.log(0.5), maxval=math.log(2.0)))
    jitter = jax.random.uniform(streams[4], (TRACES, HEADS, shard_count, L_DEV), minval=0.5, maxval=1.5)
    symbol_occurrence_tally = (base_rate * shard_factor * jitter).reshape(TRACES, HEADS, SEQ)
    places = jax.random.randint(streams[5], (TRACES, 1, 1, 2), 0, SEQ)
    input_magnitude = jnp.log(jax.random.uniform(streams[6], (TRACES, HEADS, 1, 2), minval=0.5, maxval=0.8))
    hit_indices = jnp.arange(SEQ)[None, None, :, None] == places
    spike_clusters = jnp.sum(jnp.where(hit_indices, input_magnitude, 0.0), axis=3)
    return (spike_clusters - symbol_occurrence_tally).astype(jnp.float32)


def shard_levels(stream_key, extent, cuts, smallest, top_value):
    factor_of = 1.0
    for axis_at, blocks in cuts:
        steps = jax.random.uniform(jax.random.fold_in(jax.random.fold_in(stream_key, 6), axis_at), (blocks,), jnp.float32, smallest / len(cuts), top_value / len(cuts))
        factor_of = factor_of * jnp.repeat(jnp.exp(steps), extent[axis_at] // blocks).reshape((-1,) + (1,) * (len(extent) - 1 - axis_at))
    return factor_of


def profile(amount, total, reach, lean):
    loads = [(1 << 20) // math.isqrt(standing ** lean) + 1 for standing in range(2, amount + 1)]
    surplus, given = total - reach - (amount - 1), [1] * (amount - 1)
    while surplus > 0:
        candidates = [i for i in range(amount - 1) if given[i] < reach]
        mass, budget = sum([loads[i] for i in candidates]), surplus
        for i in candidates:
            extra = min(reach - given[i], max(1, budget * loads[i] // mass), surplus)
            given[i] = given[i] + extra
            surplus = surplus - extra
    return np.array([reach] + given)


def ragged(key, count, total, most, lean):
    if count == 2:
        one = jax.random.randint(key, (), max(1, total - most), min(most, total - 1) + 1)
        return jnp.stack([one, total - one])
    lengths = jnp.asarray(profile(count, total, most, lean), jnp.int32)
    couples = (count - 1) // 2
    giver, sink = lengths[1:1 + 2 * couples:2], lengths[2:2 + 2 * couples:2]
    room = jnp.minimum(giver - 1, most - sink)
    shifted = jax.random.randint(jax.random.fold_in(key, 1), (couples,), 0, 1 << 20) % (room + 1)
    lengths = lengths.at[1:1 + 2 * couples:2].set(giver - shifted).at[2:2 + 2 * couples:2].set(sink + shifted)
    return lengths[jax.random.permutation(jax.random.fold_in(key, 2), count)]


def bell_draw(rng, extent, deviation, bound, shards=(), kind=jnp.bfloat16):
    values = jax.random.normal(rng, extent, jnp.float32) * deviation
    if len(shards) > 0:
        values = shard_levels(rng, extent, shards, -0.22, 0.18) * values
    return jnp.clip(values, min=-bound, max=bound).astype(kind)


def setup_inputs(seed: int = 0, part: int = 0) -> dict:
    seeds = jax.random.split(jax.random.key(seed), 8)
    part_keys = jax.random.split(jax.random.fold_in(seeds[7], part), 8)
    layer_input = bell_draw(part_keys[0], (TRACES, SEQ, D), 1.0, 6.0, ((0, 2), (2, 8)))
    read_weight = bell_draw(seeds[1], (D, N), D ** -0.5, 0.125, ((0, 8),))
    head_inputs = bell_draw(part_keys[2], (TRACES, SEQ, HP), 1.0, 6.0, ((0, 2), (2, 8)))
    write_vectors = bell_draw(part_keys[3], (TRACES, SEQ, N), 0.0006, 0.0034179688, ((0, 2),))
    log_decay = draw_log_decay(jax.random.fold_in(jax.random.fold_in(seeds[7], part), 71), part)
    segment_ids = jax.vmap(lambda own: jnp.searchsorted(jnp.cumsum(ragged(own, 4, SEQ, SEQ // 2, 0)), jnp.arange(SEQ), side="right"))(jax.random.split(part_keys[5], TRACES)).reshape((TRACES, SEQ)).astype(jnp.int32)
    out_grad = bell_draw(part_keys[6], (TRACES, SEQ, HP), 0.0005, 0.0029296875, ((0, 2), (2, 8)))
    return dict(layer_input=layer_input, read_weight=read_weight, head_inputs=head_inputs, write_vectors=write_vectors, log_decay=log_decay, segment_ids=segment_ids, out_grad=out_grad)


def trace_pass(readout, values, write_rows, decays, seg_rows, grads):
    block_count = SEQ // BLOCK_LEN
    group_heads = HEADS // N_MDL
    read_blocks = readout.reshape(block_count, BLOCK_LEN, N)
    value_blocks = values.reshape(block_count, BLOCK_LEN, HEADS, P_SIZE)
    key_blocks = write_rows.reshape(block_count, BLOCK_LEN, N)
    decay_blocks = jnp.moveaxis(decays.reshape(HEADS, block_count, BLOCK_LEN), 1, 0)
    seg_blocks = seg_rows.reshape(block_count, BLOCK_LEN)
    grad_blocks = grads.reshape(block_count, BLOCK_LEN, HEADS, P_SIZE)
    causal = jnp.arange(BLOCK_LEN)[:, None] >= jnp.arange(BLOCK_LEN)[None, :]

    def advance(running, pieces):
        prior_seg, state_stack = running
        read_rows, value_rows, key_rows, decay_rows, segs_here, grad_rows = pieces
        cumulative = jnp.cumsum(decay_rows, axis=1)
        allowed = jnp.logical_and(causal, segs_here[:, None] == segs_here[None, :])
        spread = cumulative[:, :, None] - cumulative[:, None, :]
        weight = jnp.where(allowed[None], jnp.exp(jnp.where(allowed[None], spread, 0.0)), 0.0)
        scores = jnp.dot(read_rows, key_rows.T, preferred_element_type=jnp.float32)
        blend_factor = (weight * scores[None]).astype(jnp.bfloat16)
        value_wide = value_rows.astype(jnp.float32)
        inside = jnp.einsum("hts,shp->thp", blend_factor.astype(jnp.float32), value_wide)
        entry = jnp.exp(cumulative) * (segs_here == prior_seg).astype(jnp.float32)[None, :]
        entry_rows = entry.T[:, :, None]
        read_wide = read_rows.astype(jnp.float32)
        states_low = state_stack.astype(jnp.bfloat16).astype(jnp.float32)
        carried = jnp.einsum("tn,hpn->thp", read_wide, states_low) * entry_rows
        result = (inside + carried).astype(jnp.bfloat16)
        grad_wide = grad_rows.astype(jnp.float32)
        products = jnp.einsum("thp,shp->hts", grad_wide, value_wide)
        grouped = (weight * products).reshape(N_MDL, group_heads, BLOCK_LEN, BLOCK_LEN)
        response = jnp.sum(grouped, axis=1).astype(jnp.bfloat16)
        readback = jnp.einsum("gts,sn->gtn", response.astype(jnp.float32), key_rows.astype(jnp.float32))
        per_head = jnp.einsum("thp,hpn->thn", grad_wide, states_low) * entry_rows
        per_group = jnp.sum(per_head.reshape(BLOCK_LEN, N_MDL, group_heads, N), axis=2)
        readback = readback + jnp.transpose(per_group, (1, 0, 2))
        back_low = readback.astype(jnp.bfloat16)
        end_weight = jnp.exp(cumulative[:, -1:] - cumulative) * (segs_here == segs_here[-1]).astype(jnp.float32)[None, :]
        weighted = (value_wide * end_weight.T[:, :, None]).astype(jnp.bfloat16)
        local_state = jnp.einsum("shp,sn->hpn", weighted.astype(jnp.float32), key_rows.astype(jnp.float32))
        linked = jnp.logical_and(segs_here[0] == segs_here[-1], segs_here[0] == prior_seg).astype(jnp.float32)
        retain = jnp.exp(cumulative[:, -1]) * linked
        state_stack = local_state + retain[:, None, None] * state_stack
        return (segs_here[-1], state_stack), (result, back_low)

    initial = (jnp.int32(-1), jnp.zeros((HEADS, P_SIZE, N), jnp.float32))
    ignored, stacked = lax.scan(advance, initial, (read_blocks, value_blocks, key_blocks, decay_blocks, seg_blocks, grad_blocks))
    outputs, readbacks = stacked
    back_wide = lax.optimization_barrier(readbacks).astype(jnp.float32)
    back_total = jnp.sum(back_wide, axis=1)
    return outputs.reshape(SEQ, HEADS * P_SIZE), back_total.reshape(SEQ, N)


def reference(layer_input, read_weight, head_inputs, write_vectors, log_decay, segment_ids, out_grad):
    flat_input = layer_input.reshape(TRACES * SEQ, D)
    share = D // N_MDL
    grouped_input = flat_input.reshape(TRACES * SEQ, N_MDL, share).astype(jnp.float32)
    grouped_weight = read_weight.reshape(N_MDL, share, N).astype(jnp.float32)
    partial_low = jnp.einsum("rgd,gdn->rgn", grouped_input, grouped_weight).astype(jnp.bfloat16)
    partial_wide = lax.optimization_barrier(partial_low).astype(jnp.float32)
    readout = jnp.sum(partial_wide, axis=1).astype(jnp.bfloat16)
    readout = readout.reshape(TRACES, SEQ, N)
    outputs = []
    readbacks = []
    for member in range(TRACES):
        result, readback = trace_pass(readout[member], head_inputs[member], write_vectors[member], log_decay[member], segment_ids[member], out_grad[member])
        outputs.append(result)
        readbacks.append(readback)
    head_outputs = jnp.stack(outputs)
    read_back = jnp.stack(readbacks).reshape(TRACES * SEQ, N).astype(jnp.bfloat16)
    read_grad = jnp.dot(read_back.T, flat_input, preferred_element_type=jnp.float32)
    return head_outputs, read_grad
```

```python
import jax
import jax.numpy as jnp
from jax import lax
from jax.experimental import pallas as pl
from jax.experimental.pallas import tpu as pltpu
from jax.sharding import PartitionSpec as P

BLOCK_LEN = 512
MESH = pl.DeviceIdType.MESH
MDL = 8
SHARE = 2 * BLOCK_LEN // MDL
HALF = BLOCK_LEN // MDL
HEAD_N = 10
PAIRS = HEAD_N // 2
TILE = 256
LOG2E = 1.4426950408889634


def shifted(value, axis, by):
    count = lax.axis_size(axis)
    pairs = [(i, i + by) for i in range(count) if 0 <= i + by < count]
    return lax.ppermute(value, axis, pairs)


def join_parts(earlier, later):
    early_first, early_last, early_pass, leading_state = earlier
    later_first, later_last, later_pass, later_state = later
    linked = jnp.logical_or(
        early_last == later_first, jnp.logical_or(early_last < 0.0, later_first < 0.0)
    )
    carried = later_pass * linked.astype(jnp.float32)[..., None]
    front_seg = jnp.where(early_first < 0.0, later_first, early_first)
    back_seg = jnp.where(later_last < 0.0, early_last, later_last)
    return (
        front_seg,
        back_seg,
        early_pass * carried,
        later_state + carried[..., None, None] * leading_state,
    )


def per_device(
    layer_input, read_weight, head_inputs, write_vectors, log_decay, segment_ids, out_grad
):
    trace_count, length, model_cols = layer_input.shape
    head_count = log_decay.shape[1]
    head_dim = head_inputs.shape[2] // head_count
    state_dim = write_vectors.shape[2]
    block_count = length // BLOCK_LEN
    rows_all = trace_count * length
    flat_count = trace_count * block_count
    flat_input = layer_input.reshape(rows_all, model_cols)
    partial_value = jnp.dot(flat_input, read_weight, preferred_element_type=jnp.float32)
    readout = lax.psum(partial_value.astype(jnp.bfloat16), "mdl")
    segments = segment_ids.astype(jnp.float32).reshape(trace_count, block_count, BLOCK_LEN)
    decays = log_decay.reshape(trace_count, head_count, block_count, BLOCK_LEN)
    positions = jnp.arange(BLOCK_LEN)
    upper = (positions[:, None] <= positions[None, :]).astype(jnp.float32)
    cumulative = jnp.einsum("bhks,st->bhkt", decays, upper, precision=lax.Precision.HIGHEST)
    closing = cumulative[..., -1:]
    at_end = (segments == segments[..., -1:]).astype(jnp.float32)
    end_weight = jnp.exp(closing - cumulative) * at_end[:, None]
    values = head_inputs.reshape(trace_count, block_count, BLOCK_LEN, head_count, head_dim)
    keys_block = write_vectors.reshape(trace_count, block_count, BLOCK_LEN, state_dim)
    weighted = (values * jnp.transpose(end_weight, (0, 2, 3, 1))[..., None]).astype(jnp.bfloat16)
    block_states = jnp.einsum(
        "bkqhp,bkqn->kbhpn", weighted, keys_block, preferred_element_type=jnp.float32
    )
    front_seg = jnp.transpose(segments[..., 0])
    back_seg = jnp.transpose(segments[..., -1])
    single = (front_seg == back_seg).astype(jnp.float32)
    through = jnp.exp(jnp.transpose(closing[..., 0], (2, 0, 1))) * single[..., None]
    neutral = (
        -jnp.ones((trace_count,), jnp.float32),
        -jnp.ones((trace_count,), jnp.float32),
        jnp.ones((trace_count, head_count), jnp.float32),
        jnp.zeros((trace_count, head_count, head_dim, state_dim), jnp.float32),
    )

    def absorb(running, pieces):
        return (join_parts(running, pieces), running)

    device_total, prefixes = lax.scan(absorb, neutral, (front_seg, back_seg, through, block_states))
    position = lax.axis_index("ctx")

    def relay_once(iteration, incoming):
        outgoing = join_parts(incoming, device_total)
        shifted_lines = shifted((outgoing[0], outgoing[1], outgoing[2], outgoing[3]), "ctx", 1)
        return tuple(
            (
                jnp.where(position == 0, anchor, arrived)
                for anchor, arrived in zip(neutral, shifted_lines)
            )
        )

    entering = lax.fori_loop(0, lax.axis_size("ctx") - 1, relay_once, neutral)
    starts = join_parts(entering, prefixes)
    start_low = starts[3].astype(jnp.bfloat16)
    prior_seg = jnp.transpose(starts[1])
    coupled_items = (segments == prior_seg[..., None]).astype(jnp.float32)
    entry_gain = jnp.exp(cumulative) * coupled_items[:, None]
    gain_rows = jnp.transpose(entry_gain, (0, 2, 3, 1))[..., None]
    readout_block = readout.reshape(trace_count, block_count, BLOCK_LEN, state_dim)
    grads_block = out_grad.reshape(trace_count, block_count, BLOCK_LEN, head_count, head_dim)
    carried_out = (
        jnp.einsum(
            "bkqn,kbhpn->bkqhp", readout_block, start_low, preferred_element_type=jnp.float32
        )
        * gain_rows
    )
    per_head = jnp.einsum(
        "bkqhp,kbhpn->bkqhn", grads_block, start_low, preferred_element_type=jnp.float32
    )
    carried_back = jnp.sum(per_head * gain_rows, axis=3)
    causal = positions[:, None] >= positions[None, :]

    def inside(pieces):
        read_rows, key_rows, value_rows, grad_rows, cum_rows, seg_rows = pieces
        allowed = jnp.logical_and(causal, seg_rows[:, None] == seg_rows[None, :])
        spread = cum_rows[:, :, None] - cum_rows[:, None, :]
        weight = jnp.where(allowed[None], jnp.exp(jnp.where(allowed[None], spread, 0.0)), 0.0)
        scores = jnp.einsum("tn,sn->ts", read_rows, key_rows, preferred_element_type=jnp.float32)
        blend_factor = (weight * scores[None]).astype(jnp.bfloat16)
        inside_out = jnp.einsum(
            "hts,shp->thp", blend_factor, value_rows, preferred_element_type=jnp.float32
        )
        products = jnp.einsum(
            "thp,shp->hts", grad_rows, value_rows, preferred_element_type=jnp.float32
        )
        response = jnp.sum(weight * products, axis=0).astype(jnp.bfloat16)
        inside_back = jnp.dot(response, key_rows, preferred_element_type=jnp.float32)
        return (inside_out, inside_back)

    own_out, own_back = lax.map(
        inside,
        (
            readout_block.reshape(flat_count, BLOCK_LEN, state_dim),
            keys_block.reshape(flat_count, BLOCK_LEN, state_dim),
            values.reshape(flat_count, BLOCK_LEN, head_count, head_dim),
            grads_block.reshape(flat_count, BLOCK_LEN, head_count, head_dim),
            jnp.transpose(cumulative, (0, 2, 1, 3)).reshape(flat_count, head_count, BLOCK_LEN),
            segments.reshape(flat_count, BLOCK_LEN),
        ),
    )
    total_out = (
        own_out.reshape(trace_count, block_count, BLOCK_LEN, head_count, head_dim) + carried_out
    )
    head_outputs = total_out.astype(jnp.bfloat16).reshape(
        trace_count, length, head_count * head_dim
    )
    back_part = (
        own_back.reshape(trace_count, block_count, BLOCK_LEN, state_dim) + carried_back
    ).reshape(rows_all, state_dim)
    read_back = lax.psum(back_part.astype(jnp.bfloat16), "mdl")
    read_grad = lax.psum_scatter(
        lax.dot_general(
            read_back, flat_input, (((0,), (0,)), ((), ())), preferred_element_type=jnp.float32
        ),
        ("ctx", "dp"),
        scatter_dimension=0,
        tiled=True,
    )
    return (head_outputs, read_grad)


def fused_kernel(
    x_ref, w_ref, hi_ref, wv_ref, ld_ref, seg_ref, og_ref, out_ref, grad_ref,
    part, rs1, readout, back, rs2, rb, gfull, grecv,
    split, stack, rowx, colx, endx, entx, bias, resp, scores, start, carry,
    rs1_s, rs1_r, ag1_s, ag1_r, rs2_s, rs2_r, ag2_s, ag2_r, dp_s, dp_r,
):
    f32, bf16 = jnp.float32, jnp.bfloat16
    me = lax.axis_index("mdl")
    core = lax.axis_index("dp")
    peers = [lax.rem(me + o, MDL) for o in range(MDL)]
    barrier = pltpu.get_barrier_semaphore()
    for o in range(1, MDL):
        pl.semaphore_signal(barrier, inc=1, device_id={"mdl": peers[o]}, device_id_type=MESH)
    pl.semaphore_signal(barrier, inc=1, device_id={"dp": 1 - core}, device_id_type=MESH)

    def remote(src, dst, send, recv, to):
        copy = pltpu.make_async_remote_copy(
            src_ref=src, dst_ref=dst, send_sem=send, recv_sem=recv,
            device_id=to, device_id_type=MESH,
        )
        copy.start()
        return copy

    part[...] = jnp.dot(x_ref[...], w_ref[...], preferred_element_type=f32).astype(bf16)
    pl.semaphore_wait(barrier, MDL)
    first = [
        remote(
            part.at[pl.ds(pl.multiple_of(peers[o] * SHARE, SHARE), SHARE)], rs1.at[o],
            rs1_s.at[o], rs1_r.at[o], {"mdl": peers[o]},
        )
        for o in range(1, MDL)
    ]

    lane = lax.broadcasted_iota(jnp.int32, (1, 128), 1)
    left = lane < 64
    mask_a = left.astype(f32).astype(bf16)
    mask_b = (1.0 - left.astype(f32)).astype(bf16)
    rows_i = lax.broadcasted_iota(jnp.int32, (BLOCK_LEN, BLOCK_LEN), 0)
    cols_i = lax.broadcasted_iota(jnp.int32, (BLOCK_LEN, BLOCK_LEN), 1)
    upper = (rows_i <= cols_i).astype(f32).astype(bf16)
    nn = (((1,), (1,)), ((), ()))
    tt = (((0,), (0,)), ((), ()))

    def prepare(k):
        span = pl.ds(k * BLOCK_LEN, BLOCK_LEN)
        split[...] = jnp.zeros_like(split)
        stack[...] = jnp.zeros_like(stack)
        rest = ld_ref[0, :, span]
        for piece in range(3):
            high = rest.astype(bf16).astype(f32)
            split[pl.ds(16 * piece, HEAD_N), :] = high
            rest = rest - high
        sums = jnp.dot(split[...].astype(bf16), upper, preferred_element_type=f32)
        cum = (sums[0:16] + sums[16:32] + sums[32:48]) * LOG2E
        seg = seg_ref[:, span].astype(f32)
        stack[pl.ds(0, 16), :] = cum
        if k == 0:
            close = cum[:, BLOCK_LEN - 1 :]
            at_end = (seg == seg[:, BLOCK_LEN - 1 :]).astype(f32)
            stack[pl.ds(16, 16), :] = jnp.exp2(close - cum) * at_end
        else:
            prior = seg_ref[:, pl.ds(BLOCK_LEN - 128, 128)].astype(f32)[:, 127:]
            stack[pl.ds(32, 16), :] = jnp.exp2(cum) * (seg == prior).astype(f32)
        stack[pl.ds(48, 8), :] = jnp.broadcast_to(seg, (8, BLOCK_LEN))
        turned = stack[...].T
        for h in range(HEAD_N):
            rowx[k, h] = cum[h : h + 1, :]
            colx[k, h] = jnp.broadcast_to(turned[:, h : h + 1], (BLOCK_LEN, 128))
        for j in range(PAIRS):
            base, target = (16, endx) if k == 0 else (32, entx)
            a = turned[:, base + 2 * j : base + 2 * j + 1]
            b = turned[:, base + 2 * j + 1 : base + 2 * j + 2]
            target[j] = jnp.where(left, a, b)
        same = jnp.logical_and(turned[:, 48:49] == seg, rows_i >= cols_i)
        bias[k] = jnp.where(same, 0.0, -1e30)

    def weight(k, h, i, wide):
        rows = pl.ds(i * TILE, TILE)
        col = colx[k, h, rows, :]
        col = jnp.concatenate([col] * (wide // 128), axis=1)
        return jnp.exp2((col - rowx[k, h, :, pl.ds(0, wide)]) + bias[k, rows, pl.ds(0, wide)])

    def lanes_of(j):
        return pl.ds(pl.multiple_of(j * 128, 128), 128)

    def backward(k):
        resp[...] = jnp.zeros_like(resp)
        carry[...] = jnp.zeros_like(carry)
        keys = wv_ref[0, pl.ds(k * BLOCK_LEN, BLOCK_LEN), :]

        def body(j, _):
            lanes = lanes_of(j)
            if k == 0:
                value = hi_ref[0, pl.ds(0, BLOCK_LEN), lanes].astype(f32)
                low = (value * endx[j]).astype(bf16)
                start[j] = lax.dot_general(low, keys, tt, preferred_element_type=f32).astype(bf16)
            else:
                grads = og_ref[0, pl.ds(BLOCK_LEN, BLOCK_LEN), lanes].astype(f32)
                carry[...] += jnp.dot(
                    (grads * entx[j]).astype(bf16), start[j], preferred_element_type=f32
                )
            for i in range(BLOCK_LEN // TILE):
                wide = (i + 1) * TILE
                value = hi_ref[0, pl.ds(k * BLOCK_LEN, wide), lanes]
                grads = og_ref[0, pl.ds(k * BLOCK_LEN + i * TILE, TILE), lanes]
                pa = lax.dot_general(grads * mask_a, value, nn, preferred_element_type=f32)
                pb = lax.dot_general(grads * mask_b, value, nn, preferred_element_type=f32)
                resp[pl.ds(i * TILE, TILE), pl.ds(0, wide)] += (
                    weight(k, 2 * j, i, wide) * pa + weight(k, 2 * j + 1, i, wide) * pb
                )
            return 0

        lax.fori_loop(0, PAIRS, body, 0)
        total = jnp.dot(resp[...].astype(bf16), keys, preferred_element_type=f32) + carry[...]
        back[pl.ds(k * BLOCK_LEN, BLOCK_LEN), :] = total.astype(bf16)
        return [
            remote(
                back.at[pl.ds(pl.multiple_of(k * BLOCK_LEN + peers[o] * HALF, HALF), HALF)],
                rs2.at[k, o], rs2_s.at[k, o], rs2_r.at[k, o], {"mdl": peers[o]},
            )
            for o in range(1, MDL)
        ]

    def forward(k):
        keys = wv_ref[0, pl.ds(k * BLOCK_LEN, BLOCK_LEN), :]
        reads = readout[pl.ds(k * BLOCK_LEN, BLOCK_LEN), :]
        scores[...] = lax.dot_general(reads, keys, nn, preferred_element_type=f32)

        def body(j, _):
            lanes = lanes_of(j)
            for i in range(BLOCK_LEN // TILE):
                wide = (i + 1) * TILE
                value = hi_ref[0, pl.ds(k * BLOCK_LEN, wide), lanes]
                score = scores[pl.ds(i * TILE, TILE), pl.ds(0, wide)]
                oa = jnp.dot(
                    (weight(k, 2 * j, i, wide) * score).astype(bf16), value,
                    preferred_element_type=f32,
                )
                ob = jnp.dot(
                    (weight(k, 2 * j + 1, i, wide) * score).astype(bf16), value,
                    preferred_element_type=f32,
                )
                total = jnp.where(left, oa, ob)
                if k == 1:
                    carried = lax.dot_general(
                        readout[pl.ds(BLOCK_LEN + i * TILE, TILE), :], start[j], nn,
                        preferred_element_type=f32,
                    )
                    total = total + carried * entx[j, pl.ds(i * TILE, TILE), :]
                out_ref[0, pl.ds(k * BLOCK_LEN + i * TILE, TILE), lanes] = total.astype(bf16)
            return 0

        lax.fori_loop(0, PAIRS, body, 0)

    def collect(k, copies):
        mine = pl.ds(pl.multiple_of(k * BLOCK_LEN + me * HALF, HALF), HALF)
        total = back[mine, :].astype(f32)
        for o in range(1, MDL):
            copies[o - 1].wait_recv()
            total = total + rs2[k, o].astype(f32)
        rb[mine, :] = total.astype(bf16)
        return [
            remote(rb.at[mine], rb.at[mine], ag2_s.at[k, o], ag2_r.at[k, o], {"mdl": peers[o]})
            for o in range(1, MDL)
        ]

    prepare(0)
    back_0 = backward(0)
    mine = pl.ds(pl.multiple_of(me * SHARE, SHARE), SHARE)
    total = part[mine, :].astype(f32)
    for o in range(1, MDL):
        first[o - 1].wait_recv()
        total = total + rs1[o].astype(f32)
    readout[mine, :] = total.astype(bf16)
    spread = [
        remote(readout.at[mine], readout.at[mine], ag1_s.at[o], ag1_r.at[o], {"mdl": peers[o]})
        for o in range(1, MDL)
    ]
    prepare(1)
    back_1 = backward(1)
    gather_0 = collect(0, back_0)
    for copy in spread:
        copy.wait_recv()
    forward(0)
    gather_1 = collect(1, back_1)
    forward(1)
    for copy in gather_0 + gather_1:
        copy.wait_recv()
    gfull[...] = lax.dot_general(rb[...], x_ref[...], tt, preferred_element_type=f32)
    owner = 1 - core
    swap = remote(
        gfull.at[pl.ds(pl.multiple_of(owner * 64, 64), 64)], grecv, dp_s, dp_r, {"dp": owner}
    )
    swap.wait_recv()
    grad_ref[...] = gfull[pl.ds(pl.multiple_of(core * 64, 64), 64), :] + grecv[...]
    swap.wait_send()
    for copy in first + spread + back_0 + back_1 + gather_0 + gather_1:
        copy.wait_send()


def fused(layer_input, read_weight, head_inputs, write_vectors, log_decay, segment_ids, out_grad):
    f32, bf16 = jnp.float32, jnp.bfloat16
    dma = pltpu.SemaphoreType.DMA
    vmem = pl.BlockSpec(memory_space=pltpu.VMEM)
    length = layer_input.shape[1]
    cols = layer_input.shape[2]
    state = write_vectors.shape[2]
    square = (BLOCK_LEN, BLOCK_LEN)
    return pl.pallas_call(
        fused_kernel,
        out_shape=(
            jax.ShapeDtypeStruct(head_inputs.shape, bf16),
            jax.ShapeDtypeStruct((state // 2, cols), f32),
        ),
        in_specs=[vmem] * 7,
        out_specs=(vmem, vmem),
        scratch_shapes=[
            pltpu.VMEM((length, state), bf16),
            pltpu.VMEM((MDL, SHARE, state), bf16),
            pltpu.VMEM((length, state), bf16),
            pltpu.VMEM((length, state), bf16),
            pltpu.VMEM((2, MDL, HALF, state), bf16),
            pltpu.VMEM((length, state), bf16),
            pltpu.VMEM((state, cols), f32),
            pltpu.VMEM((state // 2, cols), f32),
            pltpu.VMEM((48, BLOCK_LEN), f32),
            pltpu.VMEM((128, BLOCK_LEN), f32),
            pltpu.VMEM((2, HEAD_N, 1, BLOCK_LEN), f32),
            pltpu.VMEM((2, HEAD_N, BLOCK_LEN, 128), f32),
            pltpu.VMEM((PAIRS, BLOCK_LEN, 128), f32),
            pltpu.VMEM((PAIRS, BLOCK_LEN, 128), f32),
            pltpu.VMEM((2,) + square, f32),
            pltpu.VMEM(square, f32),
            pltpu.VMEM(square, f32),
            pltpu.VMEM((PAIRS, 128, state), bf16),
            pltpu.VMEM((BLOCK_LEN, state), f32),
            dma((MDL,)), dma((MDL,)), dma((MDL,)), dma((MDL,)),
            dma((2, MDL)), dma((2, MDL)), dma((2, MDL)), dma((2, MDL)),
            dma, dma,
        ],
        compiler_params=pltpu.CompilerParams(
            collective_id=0, has_side_effects=True, vmem_limit_bytes=56 * 1024 * 1024
        ),
    )(
        layer_input.reshape(length, cols), read_weight, head_inputs, write_vectors,
        log_decay, segment_ids, out_grad,
    )


def fits(mesh, values):
    (layer_input, _, head_inputs, write_vectors, log_decay, _, _) = values
    return (
        mesh.shape["ctx"] == 1
        and mesh.shape["mdl"] == MDL
        and mesh.shape["dp"] == 2
        and layer_input.shape[:2] == (1, 2 * BLOCK_LEN)
        and log_decay.shape[1] == HEAD_N
        and head_inputs.shape[2] == HEAD_N * 64
        and write_vectors.shape[2] == 128
    )


def solution(mesh):
    def chosen(*values):
        if fits(mesh, values):
            return fused(*values)
        return per_device(*values)

    placed = (
        P(("grp", "dp"), "ctx", "mdl"),
        P("mdl", None),
        P(("grp", "dp"), "ctx", "mdl"),
        P(("grp", "dp"), "ctx", None),
        P(("grp", "dp"), "mdl", "ctx"),
        P(("grp", "dp"), "ctx"),
        P(("grp", "dp"), "ctx", "mdl"),
    )
    return jax.shard_map(
        chosen,
        mesh=mesh,
        in_specs=placed,
        out_specs=(P(("grp", "dp"), "ctx", "mdl"), P(("grp", "ctx", "dp"), "mdl")),
        check_vma=False,
    )
```

```python
import jax
import jax.numpy as jnp
from jax import lax
from jax.experimental import pallas as pl
from jax.experimental.pallas import tpu as pltpu
from jax.sharding import PartitionSpec as P

BLOCK_LEN = 512
MESH = pl.DeviceIdType.MESH
MDL = 8
SHARE = 2 * BLOCK_LEN // MDL
HALF = BLOCK_LEN // MDL
HEAD_N = 10
PAIRS = HEAD_N // 2
TILE = 256
LOG2E = 1.4426950408889634


def shifted(value, axis, by):
    count = lax.axis_size(axis)
    pairs = [(i, i + by) for i in range(count) if 0 <= i + by < count]
    return lax.ppermute(value, axis, pairs)


def join_parts(earlier, later):
    early_first, early_last, early_pass, leading_state = earlier
    later_first, later_last, later_pass, later_state = later
    linked = jnp.logical_or(
        early_last == later_first, jnp.logical_or(early_last < 0.0, later_first < 0.0)
    )
    carried = later_pass * linked.astype(jnp.float32)[..., None]
    front_seg = jnp.where(early_first < 0.0, later_first, early_first)
    back_seg = jnp.where(later_last < 0.0, early_last, later_last)
    return (
        front_seg,
        back_seg,
        early_pass * carried,
        later_state + carried[..., None, None] * leading_state,
    )


def per_device(
    layer_input, read_weight, head_inputs, write_vectors, log_decay, segment_ids, out_grad
):
    trace_count, length, model_cols = layer_input.shape
    head_count = log_decay.shape[1]
    head_dim = head_inputs.shape[2] // head_count
    state_dim = write_vectors.shape[2]
    block_count = length // BLOCK_LEN
    rows_all = trace_count * length
    flat_count = trace_count * block_count
    flat_input = layer_input.reshape(rows_all, model_cols)
    partial_value = jnp.dot(flat_input, read_weight, preferred_element_type=jnp.float32)
    readout = lax.psum(partial_value.astype(jnp.bfloat16), "mdl")
    segments = segment_ids.astype(jnp.float32).reshape(trace_count, block_count, BLOCK_LEN)
    decays = log_decay.reshape(trace_count, head_count, block_count, BLOCK_LEN)
    positions = jnp.arange(BLOCK_LEN)
    upper = (positions[:, None] <= positions[None, :]).astype(jnp.float32)
    cumulative = jnp.einsum("bhks,st->bhkt", decays, upper, precision=lax.Precision.HIGHEST)
    closing = cumulative[..., -1:]
    at_end = (segments == segments[..., -1:]).astype(jnp.float32)
    end_weight = jnp.exp(closing - cumulative) * at_end[:, None]
    values = head_inputs.reshape(trace_count, block_count, BLOCK_LEN, head_count, head_dim)
    keys_block = write_vectors.reshape(trace_count, block_count, BLOCK_LEN, state_dim)
    weighted = (values * jnp.transpose(end_weight, (0, 2, 3, 1))[..., None]).astype(jnp.bfloat16)
    block_states = jnp.einsum(
        "bkqhp,bkqn->kbhpn", weighted, keys_block, preferred_element_type=jnp.float32
    )
    front_seg = jnp.transpose(segments[..., 0])
    back_seg = jnp.transpose(segments[..., -1])
    single = (front_seg == back_seg).astype(jnp.float32)
    through = jnp.exp(jnp.transpose(closing[..., 0], (2, 0, 1))) * single[..., None]
    neutral = (
        -jnp.ones((trace_count,), jnp.float32),
        -jnp.ones((trace_count,), jnp.float32),
        jnp.ones((trace_count, head_count), jnp.float32),
        jnp.zeros((trace_count, head_count, head_dim, state_dim), jnp.float32),
    )

    def absorb(running, pieces):
        return (join_parts(running, pieces), running)

    device_total, prefixes = lax.scan(absorb, neutral, (front_seg, back_seg, through, block_states))
    position = lax.axis_index("ctx")

    def relay_once(iteration, incoming):
        outgoing = join_parts(incoming, device_total)
        shifted_lines = shifted((outgoing[0], outgoing[1], outgoing[2], outgoing[3]), "ctx", 1)
        return tuple(
            (
                jnp.where(position == 0, anchor, arrived)
                for anchor, arrived in zip(neutral, shifted_lines)
            )
        )

    entering = lax.fori_loop(0, lax.axis_size("ctx") - 1, relay_once, neutral)
    starts = join_parts(entering, prefixes)
    start_low = starts[3].astype(jnp.bfloat16)
    prior_seg = jnp.transpose(starts[1])
    coupled_items = (segments == prior_seg[..., None]).astype(jnp.float32)
    entry_gain = jnp.exp(cumulative) * coupled_items[:, None]
    gain_rows = jnp.transpose(entry_gain, (0, 2, 3, 1))[..., None]
    readout_block = readout.reshape(trace_count, block_count, BLOCK_LEN, state_dim)
    grads_block = out_grad.reshape(trace_count, block_count, BLOCK_LEN, head_count, head_dim)
    carried_out = (
        jnp.einsum(
            "bkqn,kbhpn->bkqhp", readout_block, start_low, preferred_element_type=jnp.float32
        )
        * gain_rows
    )
    per_head = jnp.einsum(
        "bkqhp,kbhpn->bkqhn", grads_block, start_low, preferred_element_type=jnp.float32
    )
    carried_back = jnp.sum(per_head * gain_rows, axis=3)
    causal = positions[:, None] >= positions[None, :]

    def inside(pieces):
        read_rows, key_rows, value_rows, grad_rows, cum_rows, seg_rows = pieces
        allowed = jnp.logical_and(causal, seg_rows[:, None] == seg_rows[None, :])
        spread = cum_rows[:, :, None] - cum_rows[:, None, :]
        weight = jnp.where(allowed[None], jnp.exp(jnp.where(allowed[None], spread, 0.0)), 0.0)
        scores = jnp.einsum("tn,sn->ts", read_rows, key_rows, preferred_element_type=jnp.float32)
        blend_factor = (weight * scores[None]).astype(jnp.bfloat16)
        inside_out = jnp.einsum(
            "hts,shp->thp", blend_factor, value_rows, preferred_element_type=jnp.float32
        )
        products = jnp.einsum(
            "thp,shp->hts", grad_rows, value_rows, preferred_element_type=jnp.float32
        )
        response = jnp.sum(weight * products, axis=0).astype(jnp.bfloat16)
        inside_back = jnp.dot(response, key_rows, preferred_element_type=jnp.float32)
        return (inside_out, inside_back)

    own_out, own_back = lax.map(
        inside,
        (
            readout_block.reshape(flat_count, BLOCK_LEN, state_dim),
            keys_block.reshape(flat_count, BLOCK_LEN, state_dim),
            values.reshape(flat_count, BLOCK_LEN, head_count, head_dim),
            grads_block.reshape(flat_count, BLOCK_LEN, head_count, head_dim),
            jnp.transpose(cumulative, (0, 2, 1, 3)).reshape(flat_count, head_count, BLOCK_LEN),
            segments.reshape(flat_count, BLOCK_LEN),
        ),
    )
    total_out = (
        own_out.reshape(trace_count, block_count, BLOCK_LEN, head_count, head_dim) + carried_out
    )
    head_outputs = total_out.astype(jnp.bfloat16).reshape(
        trace_count, length, head_count * head_dim
    )
    back_part = (
        own_back.reshape(trace_count, block_count, BLOCK_LEN, state_dim) + carried_back
    ).reshape(rows_all, state_dim)
    read_back = lax.psum(back_part.astype(jnp.bfloat16), "mdl")
    read_grad = lax.psum_scatter(
        lax.dot_general(
            read_back, flat_input, (((0,), (0,)), ((), ())), preferred_element_type=jnp.float32
        ),
        ("ctx", "dp"),
        scatter_dimension=0,
        tiled=True,
    )
    return (head_outputs, read_grad)


def fused_kernel(
    x_ref, w_ref, hi_hbm, wv_ref, ld_ref, seg_ref, og_hbm, out_hbm, grad_ref,
    hi_ref, og_ref, out_ref, kept,
    part, rs1, readout, back, rs2, rb, gfull, grecv,
    split, stack, rowx, colx, endx, entx, bias, resp, scores, start, carry,
    rs1_s, rs1_r, ag1_s, ag1_r, rs2_s, rs2_r, ag2_s, ag2_r, dp_s, dp_r, in_s, out_s,
):
    f32, bf16 = jnp.float32, jnp.bfloat16
    load_hi = pltpu.make_async_copy(hi_hbm, hi_ref, in_s.at[0])
    load_og = pltpu.make_async_copy(og_hbm, og_ref, in_s.at[1])
    load_hi.start()
    load_og.start()
    me = lax.axis_index("mdl")
    core = lax.axis_index("dp")
    peers = [lax.rem(me + o, MDL) for o in range(MDL)]
    barrier = pltpu.get_barrier_semaphore()
    for o in range(1, MDL):
        pl.semaphore_signal(barrier, inc=1, device_id={"mdl": peers[o]}, device_id_type=MESH)
    pl.semaphore_signal(barrier, inc=1, device_id={"dp": 1 - core}, device_id_type=MESH)

    def remote(src, dst, send, recv, to):
        copy = pltpu.make_async_remote_copy(
            src_ref=src, dst_ref=dst, send_sem=send, recv_sem=recv,
            device_id=to, device_id_type=MESH,
        )
        copy.start()
        return copy

    nn = (((1,), (1,)), ((), ()))
    tt = (((0,), (0,)), ((), ()))
    part[...] = lax.dot_general(x_ref[...], w_ref[...], tt, preferred_element_type=f32).astype(bf16)
    pl.semaphore_wait(barrier, MDL)
    first = [
        remote(
            part.at[pl.ds(pl.multiple_of(peers[o] * SHARE, SHARE), SHARE)], rs1.at[o],
            rs1_s.at[o], rs1_r.at[o], {"mdl": peers[o]},
        )
        for o in range(1, MDL)
    ]

    lane = lax.broadcasted_iota(jnp.int32, (1, 128), 1)
    left = lane < 64
    mask_a = left.astype(f32).astype(bf16)
    mask_b = (1.0 - left.astype(f32)).astype(bf16)
    rows_i = lax.broadcasted_iota(jnp.int32, (BLOCK_LEN, BLOCK_LEN), 0)
    cols_i = lax.broadcasted_iota(jnp.int32, (BLOCK_LEN, BLOCK_LEN), 1)
    upper = (rows_i <= cols_i).astype(f32).astype(bf16)

    def prepare(k):
        span = pl.ds(k * BLOCK_LEN, BLOCK_LEN)
        split[...] = jnp.zeros_like(split)
        stack[...] = jnp.zeros_like(stack)
        for h in range(HEAD_N):
            stack[pl.ds(h, 1), :] = ld_ref[h, :, span]
        rest = stack[pl.ds(0, 16), :]
        for piece in range(3):
            high = rest.astype(bf16).astype(f32)
            split[pl.ds(16 * piece, 16), :] = high
            rest = rest - high
        sums = jnp.dot(split[...].astype(bf16), upper, preferred_element_type=f32)
        cum = (sums[0:16] + sums[16:32] + sums[32:48]) * LOG2E
        seg = seg_ref[:, span].astype(f32)
        stack[pl.ds(0, 16), :] = cum
        if k == 0:
            close = cum[:, BLOCK_LEN - 1 :]
            at_end = (seg == seg[:, BLOCK_LEN - 1 :]).astype(f32)
            stack[pl.ds(16, 16), :] = jnp.exp2(close - cum) * at_end
        else:
            prior = seg_ref[:, pl.ds(BLOCK_LEN - 128, 128)].astype(f32)[:, 127:]
            stack[pl.ds(32, 16), :] = jnp.exp2(cum) * (seg == prior).astype(f32)
        stack[pl.ds(48, 8), :] = jnp.broadcast_to(seg, (8, BLOCK_LEN))
        turned = stack[...].T
        for h in range(HEAD_N):
            rowx[k, h] = cum[h : h + 1, :]
            colx[k, h] = jnp.broadcast_to(turned[:, h : h + 1], (BLOCK_LEN, 128))
        for j in range(PAIRS):
            base, target = (16, endx) if k == 0 else (32, entx)
            a = turned[:, base + 2 * j : base + 2 * j + 1]
            b = turned[:, base + 2 * j + 1 : base + 2 * j + 2]
            target[j] = jnp.where(left, a, b)
        same = jnp.logical_and(turned[:, 48:49] == seg, rows_i >= cols_i)
        bias[k] = jnp.where(same, 0.0, -1e30)

    def weight(k, h, i, wide):
        rows = pl.ds(i * TILE, TILE)
        col = colx[k, h, rows, :]
        col = jnp.concatenate([col] * (wide // 128), axis=1)
        return jnp.exp2((col - rowx[k, h, :, pl.ds(0, wide)]) + bias[k, rows, pl.ds(0, wide)])

    def lanes_of(j):
        return pl.ds(pl.multiple_of(j * 128, 128), 128)

    def backward(k):
        resp[...] = jnp.zeros_like(resp)
        carry[...] = jnp.zeros_like(carry)
        keys = wv_ref[0, pl.ds(k * BLOCK_LEN, BLOCK_LEN), :]

        def body(j, _):
            lanes = lanes_of(j)
            if k == 0:
                value = hi_ref[0, pl.ds(0, BLOCK_LEN), lanes].astype(f32)
                low = (value * endx[j]).astype(bf16)
                start[j] = lax.dot_general(low, keys, tt, preferred_element_type=f32).astype(bf16)
            else:
                grads = og_ref[0, pl.ds(BLOCK_LEN, BLOCK_LEN), lanes].astype(f32)
                carry[...] += jnp.dot(
                    (grads * entx[j]).astype(bf16), start[j], preferred_element_type=f32
                )
            for i in range(BLOCK_LEN // TILE):
                wide = (i + 1) * TILE
                value = hi_ref[0, pl.ds(k * BLOCK_LEN, wide), lanes]
                grads = og_ref[0, pl.ds(k * BLOCK_LEN + i * TILE, TILE), lanes]
                pa = lax.dot_general(grads * mask_a, value, nn, preferred_element_type=f32)
                pb = lax.dot_general(grads * mask_b, value, nn, preferred_element_type=f32)
                wa = weight(k, 2 * j, i, wide)
                wb = weight(k, 2 * j + 1, i, wide)
                rows = pl.ds(i * TILE, TILE)
                kept[k, 2 * j, rows, pl.ds(0, wide)] = wa.astype(bf16)
                kept[k, 2 * j + 1, rows, pl.ds(0, wide)] = wb.astype(bf16)
                resp[rows, pl.ds(0, wide)] += wa * pa + wb * pb
            return 0

        lax.fori_loop(0, PAIRS, body, 0)
        total = jnp.dot(resp[...].astype(bf16), keys, preferred_element_type=f32) + carry[...]
        back[pl.ds(k * BLOCK_LEN, BLOCK_LEN), :] = total.astype(bf16)
        return [
            remote(
                back.at[pl.ds(pl.multiple_of(k * BLOCK_LEN + peers[o] * HALF, HALF), HALF)],
                rs2.at[k, o], rs2_s.at[k, o], rs2_r.at[k, o], {"mdl": peers[o]},
            )
            for o in range(1, MDL)
        ]

    def forward(k):
        keys = wv_ref[0, pl.ds(k * BLOCK_LEN, BLOCK_LEN), :]
        reads = readout[pl.ds(k * BLOCK_LEN, BLOCK_LEN), :]
        scores[...] = lax.dot_general(reads, keys, nn, preferred_element_type=f32).astype(bf16)

        def body(j, _):
            lanes = lanes_of(j)
            for i in range(BLOCK_LEN // TILE):
                wide = (i + 1) * TILE
                value = hi_ref[0, pl.ds(k * BLOCK_LEN, wide), lanes]
                rows = pl.ds(i * TILE, TILE)
                score = scores[rows, pl.ds(0, wide)]
                mix_a = kept[k, 2 * j, rows, pl.ds(0, wide)] * score
                mix_b = kept[k, 2 * j + 1, rows, pl.ds(0, wide)] * score
                oa = jnp.dot(mix_a, value, preferred_element_type=f32)
                ob = jnp.dot(mix_b, value, preferred_element_type=f32)
                total = jnp.where(left, oa, ob)
                if k == 1:
                    carried = lax.dot_general(
                        readout[pl.ds(BLOCK_LEN + i * TILE, TILE), :], start[j], nn,
                        preferred_element_type=f32,
                    )
                    total = total + carried * entx[j, pl.ds(i * TILE, TILE), :]
                out_ref[0, pl.ds(k * BLOCK_LEN + i * TILE, TILE), lanes] = total.astype(bf16)
            return 0

        lax.fori_loop(0, PAIRS, body, 0)
        span = pl.ds(k * BLOCK_LEN, BLOCK_LEN)
        store = pltpu.make_async_copy(out_ref.at[:, span], out_hbm.at[:, span], out_s.at[k])
        store.start()
        return store

    def collect(k, copies):
        mine = pl.ds(pl.multiple_of(k * BLOCK_LEN + me * HALF, HALF), HALF)
        total = back[mine, :].astype(f32)
        for o in range(1, MDL):
            copies[o - 1].wait_recv()
            total = total + rs2[k, o].astype(f32)
        rb[mine, :] = total.astype(bf16)
        return [
            remote(rb.at[mine], rb.at[mine], ag2_s.at[k, o], ag2_r.at[k, o], {"mdl": peers[o]})
            for o in range(1, MDL)
        ]

    prepare(0)
    load_hi.wait()
    load_og.wait()
    back_0 = backward(0)
    mine = pl.ds(pl.multiple_of(me * SHARE, SHARE), SHARE)
    total = part[mine, :].astype(f32)
    for o in range(1, MDL):
        first[o - 1].wait_recv()
        total = total + rs1[o].astype(f32)
    readout[mine, :] = total.astype(bf16)
    spread = [
        remote(readout.at[mine], readout.at[mine], ag1_s.at[o], ag1_r.at[o], {"mdl": peers[o]})
        for o in range(1, MDL)
    ]
    prepare(1)
    back_1 = backward(1)
    gather_0 = collect(0, back_0)
    for copy in spread:
        copy.wait_recv()
    store_0 = forward(0)
    gather_1 = collect(1, back_1)
    store_1 = forward(1)
    for copy in gather_0 + gather_1:
        copy.wait_recv()
    gfull[...] = lax.dot_general(rb[...], x_ref[...], (((0,), (1,)), ((), ())), preferred_element_type=f32)
    owner = 1 - core
    swap = remote(
        gfull.at[pl.ds(pl.multiple_of(owner * 64, 64), 64)], grecv, dp_s, dp_r, {"dp": owner}
    )
    swap.wait_recv()
    grad_ref[...] = gfull[pl.ds(pl.multiple_of(core * 64, 64), 64), :] + grecv[...]
    swap.wait_send()
    store_0.wait()
    store_1.wait()
    for copy in first + spread + back_0 + back_1 + gather_0 + gather_1:
        copy.wait_send()


def fused(layer_input, read_weight, head_inputs, write_vectors, log_decay, segment_ids, out_grad):
    f32, bf16 = jnp.float32, jnp.bfloat16
    dma = pltpu.SemaphoreType.DMA
    vmem = pl.BlockSpec(memory_space=pltpu.VMEM)
    anywhere = pl.BlockSpec(memory_space=pl.ANY)
    length = layer_input.shape[1]
    cols = layer_input.shape[2]
    state = write_vectors.shape[2]
    square = (BLOCK_LEN, BLOCK_LEN)
    return pl.pallas_call(
        fused_kernel,
        out_shape=(
            jax.ShapeDtypeStruct(head_inputs.shape, bf16),
            jax.ShapeDtypeStruct((state // 2, cols), f32),
        ),
        in_specs=[vmem, vmem, anywhere, vmem, vmem, vmem, anywhere],
        out_specs=(anywhere, vmem),
        scratch_shapes=[
            pltpu.VMEM(head_inputs.shape, bf16),
            pltpu.VMEM(head_inputs.shape, bf16),
            pltpu.VMEM(head_inputs.shape, bf16),
            pltpu.VMEM((2, HEAD_N) + square, bf16),
            pltpu.VMEM((length, state), bf16),
            pltpu.VMEM((MDL, SHARE, state), bf16),
            pltpu.VMEM((length, state), bf16),
            pltpu.VMEM((length, state), bf16),
            pltpu.VMEM((2, MDL, HALF, state), bf16),
            pltpu.VMEM((length, state), bf16),
            pltpu.VMEM((state, cols), f32),
            pltpu.VMEM((state // 2, cols), f32),
            pltpu.VMEM((48, BLOCK_LEN), f32),
            pltpu.VMEM((128, BLOCK_LEN), f32),
            pltpu.VMEM((2, HEAD_N, 1, BLOCK_LEN), f32),
            pltpu.VMEM((2, HEAD_N, BLOCK_LEN, 128), f32),
            pltpu.VMEM((PAIRS, BLOCK_LEN, 128), f32),
            pltpu.VMEM((PAIRS, BLOCK_LEN, 128), f32),
            pltpu.VMEM((2,) + square, f32),
            pltpu.VMEM(square, f32),
            pltpu.VMEM(square, bf16),
            pltpu.VMEM((PAIRS, 128, state), bf16),
            pltpu.VMEM((BLOCK_LEN, state), f32),
            dma((MDL,)), dma((MDL,)), dma((MDL,)), dma((MDL,)),
            dma((2, MDL)), dma((2, MDL)), dma((2, MDL)), dma((2, MDL)),
            dma, dma, dma((2,)), dma((2,)),
        ],
        compiler_params=pltpu.CompilerParams(
            collective_id=0, has_side_effects=True, vmem_limit_bytes=56 * 1024 * 1024
        ),
    )(
        layer_input.reshape(length, cols).T, read_weight, head_inputs, write_vectors,
        jnp.transpose(log_decay, (1, 0, 2)), segment_ids, out_grad,
    )


def fits(mesh, values):
    (layer_input, _, head_inputs, write_vectors, log_decay, _, _) = values
    return (
        mesh.shape["ctx"] == 1
        and mesh.shape["mdl"] == MDL
        and mesh.shape["dp"] == 2
        and layer_input.shape[:2] == (1, 2 * BLOCK_LEN)
        and log_decay.shape[1] == HEAD_N
        and head_inputs.shape[2] == HEAD_N * 64
        and write_vectors.shape[2] == 128
    )


def solution(mesh):
    def chosen(*values):
        if fits(mesh, values):
            return fused(*values)
        return per_device(*values)

    placed = (
        P(("grp", "dp"), "ctx", "mdl"),
        P("mdl", None),
        P(("grp", "dp"), "ctx", "mdl"),
        P(("grp", "dp"), "ctx", None),
        P(("grp", "dp"), "mdl", "ctx"),
        P(("grp", "dp"), "ctx"),
        P(("grp", "dp"), "ctx", "mdl"),
    )
    return jax.shard_map(
        chosen,
        mesh=mesh,
        in_specs=placed,
        out_specs=(P(("grp", "dp"), "ctx", "mdl"), P(("grp", "ctx", "dp"), "mdl")),
        check_vma=False,
    )
```

```python
import jax
import jax.numpy as jnp
from jax import lax
from jax.experimental import pallas as pl
from jax.experimental.pallas import tpu as pltpu
from jax.sharding import PartitionSpec as P

BLOCK_LEN = 512
MESH = pl.DeviceIdType.MESH
MDL = 8
SHARE = 2 * BLOCK_LEN // MDL
HALF = BLOCK_LEN // MDL
HEAD_N = 10
PAIRS = HEAD_N // 2
TILE = 256
LOG2E = 1.4426950408889634


def shifted(value, axis, by):
    count = lax.axis_size(axis)
    pairs = [(i, i + by) for i in range(count) if 0 <= i + by < count]
    return lax.ppermute(value, axis, pairs)


def join_parts(earlier, later):
    early_first, early_last, early_pass, leading_state = earlier
    later_first, later_last, later_pass, later_state = later
    linked = jnp.logical_or(
        early_last == later_first, jnp.logical_or(early_last < 0.0, later_first < 0.0)
    )
    carried = later_pass * linked.astype(jnp.float32)[..., None]
    front_seg = jnp.where(early_first < 0.0, later_first, early_first)
    back_seg = jnp.where(later_last < 0.0, early_last, later_last)
    return (
        front_seg,
        back_seg,
        early_pass * carried,
        later_state + carried[..., None, None] * leading_state,
    )


def per_device(
    layer_input, read_weight, head_inputs, write_vectors, log_decay, segment_ids, out_grad
):
    trace_count, length, model_cols = layer_input.shape
    head_count = log_decay.shape[1]
    head_dim = head_inputs.shape[2] // head_count
    state_dim = write_vectors.shape[2]
    block_count = length // BLOCK_LEN
    rows_all = trace_count * length
    flat_count = trace_count * block_count
    flat_input = layer_input.reshape(rows_all, model_cols)
    partial_value = jnp.dot(flat_input, read_weight, preferred_element_type=jnp.float32)
    readout = lax.psum(partial_value.astype(jnp.bfloat16), "mdl")
    segments = segment_ids.astype(jnp.float32).reshape(trace_count, block_count, BLOCK_LEN)
    decays = log_decay.reshape(trace_count, head_count, block_count, BLOCK_LEN)
    positions = jnp.arange(BLOCK_LEN)
    upper = (positions[:, None] <= positions[None, :]).astype(jnp.float32)
    cumulative = jnp.einsum("bhks,st->bhkt", decays, upper, precision=lax.Precision.HIGHEST)
    closing = cumulative[..., -1:]
    at_end = (segments == segments[..., -1:]).astype(jnp.float32)
    end_weight = jnp.exp(closing - cumulative) * at_end[:, None]
    values = head_inputs.reshape(trace_count, block_count, BLOCK_LEN, head_count, head_dim)
    keys_block = write_vectors.reshape(trace_count, block_count, BLOCK_LEN, state_dim)
    weighted = (values * jnp.transpose(end_weight, (0, 2, 3, 1))[..., None]).astype(jnp.bfloat16)
    block_states = jnp.einsum(
        "bkqhp,bkqn->kbhpn", weighted, keys_block, preferred_element_type=jnp.float32
    )
    front_seg = jnp.transpose(segments[..., 0])
    back_seg = jnp.transpose(segments[..., -1])
    single = (front_seg == back_seg).astype(jnp.float32)
    through = jnp.exp(jnp.transpose(closing[..., 0], (2, 0, 1))) * single[..., None]
    neutral = (
        -jnp.ones((trace_count,), jnp.float32),
        -jnp.ones((trace_count,), jnp.float32),
        jnp.ones((trace_count, head_count), jnp.float32),
        jnp.zeros((trace_count, head_count, head_dim, state_dim), jnp.float32),
    )

    def absorb(running, pieces):
        return (join_parts(running, pieces), running)

    device_total, prefixes = lax.scan(absorb, neutral, (front_seg, back_seg, through, block_states))
    position = lax.axis_index("ctx")

    def relay_once(iteration, incoming):
        outgoing = join_parts(incoming, device_total)
        shifted_lines = shifted((outgoing[0], outgoing[1], outgoing[2], outgoing[3]), "ctx", 1)
        return tuple(
            (
                jnp.where(position == 0, anchor, arrived)
                for anchor, arrived in zip(neutral, shifted_lines)
            )
        )

    entering = lax.fori_loop(0, lax.axis_size("ctx") - 1, relay_once, neutral)
    starts = join_parts(entering, prefixes)
    start_low = starts[3].astype(jnp.bfloat16)
    prior_seg = jnp.transpose(starts[1])
    coupled_items = (segments == prior_seg[..., None]).astype(jnp.float32)
    entry_gain = jnp.exp(cumulative) * coupled_items[:, None]
    gain_rows = jnp.transpose(entry_gain, (0, 2, 3, 1))[..., None]
    readout_block = readout.reshape(trace_count, block_count, BLOCK_LEN, state_dim)
    grads_block = out_grad.reshape(trace_count, block_count, BLOCK_LEN, head_count, head_dim)
    carried_out = (
        jnp.einsum(
            "bkqn,kbhpn->bkqhp", readout_block, start_low, preferred_element_type=jnp.float32
        )
        * gain_rows
    )
    per_head = jnp.einsum(
        "bkqhp,kbhpn->bkqhn", grads_block, start_low, preferred_element_type=jnp.float32
    )
    carried_back = jnp.sum(per_head * gain_rows, axis=3)
    causal = positions[:, None] >= positions[None, :]

    def inside(pieces):
        read_rows, key_rows, value_rows, grad_rows, cum_rows, seg_rows = pieces
        allowed = jnp.logical_and(causal, seg_rows[:, None] == seg_rows[None, :])
        spread = cum_rows[:, :, None] - cum_rows[:, None, :]
        weight = jnp.where(allowed[None], jnp.exp(jnp.where(allowed[None], spread, 0.0)), 0.0)
        scores = jnp.einsum("tn,sn->ts", read_rows, key_rows, preferred_element_type=jnp.float32)
        blend_factor = (weight * scores[None]).astype(jnp.bfloat16)
        inside_out = jnp.einsum(
            "hts,shp->thp", blend_factor, value_rows, preferred_element_type=jnp.float32
        )
        products = jnp.einsum(
            "thp,shp->hts", grad_rows, value_rows, preferred_element_type=jnp.float32
        )
        response = jnp.sum(weight * products, axis=0).astype(jnp.bfloat16)
        inside_back = jnp.dot(response, key_rows, preferred_element_type=jnp.float32)
        return (inside_out, inside_back)

    own_out, own_back = lax.map(
        inside,
        (
            readout_block.reshape(flat_count, BLOCK_LEN, state_dim),
            keys_block.reshape(flat_count, BLOCK_LEN, state_dim),
            values.reshape(flat_count, BLOCK_LEN, head_count, head_dim),
            grads_block.reshape(flat_count, BLOCK_LEN, head_count, head_dim),
            jnp.transpose(cumulative, (0, 2, 1, 3)).reshape(flat_count, head_count, BLOCK_LEN),
            segments.reshape(flat_count, BLOCK_LEN),
        ),
    )
    total_out = (
        own_out.reshape(trace_count, block_count, BLOCK_LEN, head_count, head_dim) + carried_out
    )
    head_outputs = total_out.astype(jnp.bfloat16).reshape(
        trace_count, length, head_count * head_dim
    )
    back_part = (
        own_back.reshape(trace_count, block_count, BLOCK_LEN, state_dim) + carried_back
    ).reshape(rows_all, state_dim)
    read_back = lax.psum(back_part.astype(jnp.bfloat16), "mdl")
    read_grad = lax.psum_scatter(
        lax.dot_general(
            read_back, flat_input, (((0,), (0,)), ((), ())), preferred_element_type=jnp.float32
        ),
        ("ctx", "dp"),
        scatter_dimension=0,
        tiled=True,
    )
    return (head_outputs, read_grad)


def fused_kernel(
    x_ref, w_ref, hi_hbm, wv_ref, ld_ref, seg_ref, og_hbm, out_hbm, grad_ref,
    hi_ref, og_ref, out_ref, kept,
    part, rs1, readout, back, rs2, rb, gfull, grecv,
    split, stack, rowx, colx, endx, entx, bias, resp, scores, start, carry,
    rs1_s, rs1_r, ag1_s, ag1_r, rs2_s, rs2_r, ag2_s, ag2_r, dp_s, dp_r, in_s, out_s,
):
    f32, bf16 = jnp.float32, jnp.bfloat16
    load_hi = pltpu.make_async_copy(hi_hbm, hi_ref, in_s.at[0])
    load_og = pltpu.make_async_copy(og_hbm, og_ref, in_s.at[1])
    load_hi.start()
    load_og.start()
    me = lax.axis_index("mdl")
    core = lax.axis_index("dp")
    peers = [lax.rem(me + o, MDL) for o in range(MDL)]
    barrier = pltpu.get_barrier_semaphore()
    for o in range(1, MDL):
        pl.semaphore_signal(barrier, inc=1, device_id={"mdl": peers[o]}, device_id_type=MESH)
    pl.semaphore_signal(barrier, inc=1, device_id={"dp": 1 - core}, device_id_type=MESH)

    def remote(src, dst, send, recv, to):
        copy = pltpu.make_async_remote_copy(
            src_ref=src, dst_ref=dst, send_sem=send, recv_sem=recv,
            device_id=to, device_id_type=MESH,
        )
        copy.start()
        return copy

    nn = (((1,), (1,)), ((), ()))
    tt = (((0,), (0,)), ((), ()))
    part[...] = lax.dot_general(x_ref[...], w_ref[...], tt, preferred_element_type=f32).astype(bf16)
    pl.semaphore_wait(barrier, MDL)
    first = [
        remote(
            part.at[pl.ds(pl.multiple_of(peers[o] * SHARE, SHARE), SHARE)], rs1.at[o],
            rs1_s.at[o], rs1_r.at[o], {"mdl": peers[o]},
        )
        for o in range(1, MDL)
    ]

    lane = lax.broadcasted_iota(jnp.int32, (1, 128), 1)
    left = lane < 64
    mask_a = left.astype(f32).astype(bf16)
    mask_b = (1.0 - left.astype(f32)).astype(bf16)
    rows_i = lax.broadcasted_iota(jnp.int32, (BLOCK_LEN, BLOCK_LEN), 0)
    cols_i = lax.broadcasted_iota(jnp.int32, (BLOCK_LEN, BLOCK_LEN), 1)
    upper = (rows_i <= cols_i).astype(f32).astype(bf16)

    def prepare(k):
        span = pl.ds(k * BLOCK_LEN, BLOCK_LEN)
        split[...] = jnp.zeros_like(split)
        stack[...] = jnp.zeros_like(stack)
        for h in range(HEAD_N):
            stack[pl.ds(h, 1), :] = ld_ref[h, :, span]
        rest = stack[pl.ds(0, 16), :]
        for piece in range(3):
            high = rest.astype(bf16).astype(f32)
            split[pl.ds(16 * piece, 16), :] = high
            rest = rest - high
        sums = jnp.dot(split[...].astype(bf16), upper, preferred_element_type=f32)
        cum = (sums[0:16] + sums[16:32] + sums[32:48]) * LOG2E
        seg = seg_ref[:, span].astype(f32)
        stack[pl.ds(0, 16), :] = cum
        if k == 0:
            close = cum[:, BLOCK_LEN - 1 :]
            at_end = (seg == seg[:, BLOCK_LEN - 1 :]).astype(f32)
            stack[pl.ds(16, 16), :] = jnp.exp2(close - cum) * at_end
        else:
            prior = seg_ref[:, pl.ds(BLOCK_LEN - 128, 128)].astype(f32)[:, 127:]
            stack[pl.ds(32, 16), :] = jnp.exp2(cum) * (seg == prior).astype(f32)
        stack[pl.ds(48, 8), :] = jnp.broadcast_to(seg, (8, BLOCK_LEN))
        turned = stack[...].T
        for h in range(HEAD_N):
            rowx[k, h] = cum[h : h + 1, :]
            colx[k, h] = jnp.broadcast_to(turned[:, h : h + 1], (BLOCK_LEN, 128))
        for j in range(PAIRS):
            base, target = (16, endx) if k == 0 else (32, entx)
            a = turned[:, base + 2 * j : base + 2 * j + 1]
            b = turned[:, base + 2 * j + 1 : base + 2 * j + 2]
            target[j] = jnp.where(left, a, b)
        same = jnp.logical_and(turned[:, 48:49] == seg, rows_i >= cols_i)
        bias[k] = jnp.where(same, 0.0, -1e30)

    def weight(k, h, i, wide):
        rows = pl.ds(i * TILE, TILE)
        col = colx[k, h, rows, :]
        col = jnp.concatenate([col] * (wide // 128), axis=1)
        return jnp.exp2((col - rowx[k, h, :, pl.ds(0, wide)]) + bias[k, rows, pl.ds(0, wide)])

    def lanes_of(j):
        return pl.ds(pl.multiple_of(j * 128, 128), 128)

    def backward(k):
        resp[...] = jnp.zeros_like(resp)
        carry[...] = jnp.zeros_like(carry)
        keys = wv_ref[0, pl.ds(k * BLOCK_LEN, BLOCK_LEN), :]

        def body(j, _):
            lanes = lanes_of(j)
            if k == 0:
                value = hi_ref[0, pl.ds(0, BLOCK_LEN), lanes].astype(f32)
                low = (value * endx[j]).astype(bf16)
                start[j] = lax.dot_general(low, keys, tt, preferred_element_type=f32).astype(bf16)
            else:
                grads = og_ref[0, pl.ds(BLOCK_LEN, BLOCK_LEN), lanes].astype(f32)
                carry[...] += jnp.dot(
                    (grads * entx[j]).astype(bf16), start[j], preferred_element_type=f32
                )
            for i in range(BLOCK_LEN // TILE):
                wide = (i + 1) * TILE
                value = hi_ref[0, pl.ds(k * BLOCK_LEN, wide), lanes]
                grads = og_ref[0, pl.ds(k * BLOCK_LEN + i * TILE, TILE), lanes]
                pa = lax.dot_general(grads * mask_a, value, nn, preferred_element_type=f32)
                pb = lax.dot_general(grads * mask_b, value, nn, preferred_element_type=f32)
                wa = weight(k, 2 * j, i, wide)
                wb = weight(k, 2 * j + 1, i, wide)
                rows = pl.ds(i * TILE, TILE)
                kept[k, 2 * j, rows, pl.ds(0, wide)] = wa.astype(bf16)
                kept[k, 2 * j + 1, rows, pl.ds(0, wide)] = wb.astype(bf16)
                resp[rows, pl.ds(0, wide)] += wa * pa + wb * pb
            return 0

        lax.fori_loop(0, PAIRS, body, 0)
        total = jnp.dot(resp[...].astype(bf16), keys, preferred_element_type=f32) + carry[...]
        back[pl.ds(k * BLOCK_LEN, BLOCK_LEN), :] = total.astype(bf16)
        return [
            remote(
                back.at[pl.ds(pl.multiple_of(k * BLOCK_LEN + peers[o] * HALF, HALF), HALF)],
                rs2.at[k, o], rs2_s.at[k, o], rs2_r.at[k, o], {"mdl": peers[o]},
            )
            for o in range(1, MDL)
        ]

    def forward(k):
        keys = wv_ref[0, pl.ds(k * BLOCK_LEN, BLOCK_LEN), :]
        reads = readout[pl.ds(k * BLOCK_LEN, BLOCK_LEN), :]
        scores[...] = lax.dot_general(reads, keys, nn, preferred_element_type=f32).astype(bf16)

        def body(j, _):
            lanes = lanes_of(j)
            for i in range(BLOCK_LEN // TILE):
                wide = (i + 1) * TILE
                value = hi_ref[0, pl.ds(k * BLOCK_LEN, wide), lanes]
                rows = pl.ds(i * TILE, TILE)
                score = scores[rows, pl.ds(0, wide)]
                mix_a = kept[k, 2 * j, rows, pl.ds(0, wide)] * score
                mix_b = kept[k, 2 * j + 1, rows, pl.ds(0, wide)] * score
                oa = jnp.dot(mix_a, value, preferred_element_type=f32)
                ob = jnp.dot(mix_b, value, preferred_element_type=f32)
                total = jnp.where(left, oa, ob)
                if k == 1:
                    carried = lax.dot_general(
                        readout[pl.ds(BLOCK_LEN + i * TILE, TILE), :], start[j], nn,
                        preferred_element_type=f32,
                    )
                    total = total + carried * entx[j, pl.ds(i * TILE, TILE), :]
                out_ref[0, pl.ds(k * BLOCK_LEN + i * TILE, TILE), lanes] = total.astype(bf16)
            return 0

        lax.fori_loop(0, PAIRS, body, 0)
        span = pl.ds(k * BLOCK_LEN, BLOCK_LEN)
        store = pltpu.make_async_copy(out_ref.at[:, span], out_hbm.at[:, span], out_s.at[k])
        store.start()
        return store

    across = me + 1 - 2 * lax.rem(me, 2)
    lines = [lax.rem(me + 2 * q, MDL) for q in range(4)]
    origins = [lax.rem(me + MDL - 2 * q, MDL) for q in range(4)]

    def gather(ref, begin, size, send, recv):
        mine = pl.ds(pl.multiple_of(begin + me * size, size), size)
        near = [
            remote(ref.at[mine], ref.at[mine], send(q), recv(q), {"mdl": lines[q]})
            for q in (2, 3, 1)
        ]
        return near, [remote(ref.at[mine], ref.at[mine], send(4), recv(4), {"mdl": across})]

    def relay(copies, ref, begin, size, send, recv):
        near, far = copies
        for at in (2, 1, 0):
            q = (2, 3, 1)[at]
            near[at].wait_recv()
            rows = pl.ds(pl.multiple_of(begin + origins[q] * size, size), size)
            far.append(
                remote(ref.at[rows], ref.at[rows], send(4 + q), recv(4 + q), {"mdl": across})
            )
        return near + far, far

    sems_1 = (lambda o: ag1_s.at[o]), (lambda o: ag1_r.at[o])
    sems_2 = [
        ((lambda o: ag2_s.at[0, o]), (lambda o: ag2_r.at[0, o])),
        ((lambda o: ag2_s.at[1, o]), (lambda o: ag2_r.at[1, o])),
    ]

    def collect(k, copies):
        mine = pl.ds(pl.multiple_of(k * BLOCK_LEN + me * HALF, HALF), HALF)
        total = back[mine, :].astype(f32)
        for o in range(1, MDL):
            copies[o - 1].wait_recv()
            total = total + rs2[k, o].astype(f32)
        rb[mine, :] = total.astype(bf16)
        return gather(rb, k * BLOCK_LEN, HALF, *sems_2[k])

    prepare(0)
    load_hi.wait()
    load_og.wait()
    back_0 = backward(0)
    mine = pl.ds(pl.multiple_of(me * SHARE, SHARE), SHARE)
    total = part[mine, :].astype(f32)
    for o in range(1, MDL):
        first[o - 1].wait_recv()
        total = total + rs1[o].astype(f32)
    readout[mine, :] = total.astype(bf16)
    spread = gather(readout, 0, SHARE, *sems_1)
    prepare(1)
    back_1 = backward(1)
    spread, landing = relay(spread, readout, 0, SHARE, *sems_1)
    gather_0 = collect(0, back_0)
    for copy in landing:
        copy.wait_recv()
    store_0 = forward(0)
    gather_1 = collect(1, back_1)
    gather_0, landing_0 = relay(gather_0, rb, 0, HALF, *sems_2[0])
    store_1 = forward(1)
    gather_1, landing_1 = relay(gather_1, rb, BLOCK_LEN, HALF, *sems_2[1])
    for copy in landing_0 + landing_1:
        copy.wait_recv()
    gfull[...] = lax.dot_general(rb[...], x_ref[...], (((0,), (1,)), ((), ())), preferred_element_type=f32)
    owner = 1 - core
    swap = remote(
        gfull.at[pl.ds(pl.multiple_of(owner * 64, 64), 64)], grecv, dp_s, dp_r, {"dp": owner}
    )
    swap.wait_recv()
    grad_ref[...] = gfull[pl.ds(pl.multiple_of(core * 64, 64), 64), :] + grecv[...]
    swap.wait_send()
    store_0.wait()
    store_1.wait()
    for copy in first + spread + back_0 + back_1 + gather_0 + gather_1:
        copy.wait_send()


def fused(layer_input, read_weight, head_inputs, write_vectors, log_decay, segment_ids, out_grad):
    f32, bf16 = jnp.float32, jnp.bfloat16
    dma = pltpu.SemaphoreType.DMA
    vmem = pl.BlockSpec(memory_space=pltpu.VMEM)
    anywhere = pl.BlockSpec(memory_space=pl.ANY)
    length = layer_input.shape[1]
    cols = layer_input.shape[2]
    state = write_vectors.shape[2]
    square = (BLOCK_LEN, BLOCK_LEN)
    return pl.pallas_call(
        fused_kernel,
        out_shape=(
            jax.ShapeDtypeStruct(head_inputs.shape, bf16),
            jax.ShapeDtypeStruct((state // 2, cols), f32),
        ),
        in_specs=[vmem, vmem, anywhere, vmem, vmem, vmem, anywhere],
        out_specs=(anywhere, vmem),
        scratch_shapes=[
            pltpu.VMEM(head_inputs.shape, bf16),
            pltpu.VMEM(head_inputs.shape, bf16),
            pltpu.VMEM(head_inputs.shape, bf16),
            pltpu.VMEM((2, HEAD_N) + square, bf16),
            pltpu.VMEM((length, state), bf16),
            pltpu.VMEM((MDL, SHARE, state), bf16),
            pltpu.VMEM((length, state), bf16),
            pltpu.VMEM((length, state), bf16),
            pltpu.VMEM((2, MDL, HALF, state), bf16),
            pltpu.VMEM((length, state), bf16),
            pltpu.VMEM((state, cols), f32),
            pltpu.VMEM((state // 2, cols), f32),
            pltpu.VMEM((48, BLOCK_LEN), f32),
            pltpu.VMEM((128, BLOCK_LEN), f32),
            pltpu.VMEM((2, HEAD_N, 1, BLOCK_LEN), f32),
            pltpu.VMEM((2, HEAD_N, BLOCK_LEN, 128), f32),
            pltpu.VMEM((PAIRS, BLOCK_LEN, 128), f32),
            pltpu.VMEM((PAIRS, BLOCK_LEN, 128), f32),
            pltpu.VMEM((2,) + square, f32),
            pltpu.VMEM(square, f32),
            pltpu.VMEM(square, bf16),
            pltpu.VMEM((PAIRS, 128, state), bf16),
            pltpu.VMEM((BLOCK_LEN, state), f32),
            dma((MDL,)), dma((MDL,)), dma((MDL,)), dma((MDL,)),
            dma((2, MDL)), dma((2, MDL)), dma((2, MDL)), dma((2, MDL)),
            dma, dma, dma((2,)), dma((2,)),
        ],
        compiler_params=pltpu.CompilerParams(
            collective_id=0, has_side_effects=True, vmem_limit_bytes=56 * 1024 * 1024
        ),
    )(
        layer_input.reshape(length, cols).T, read_weight, head_inputs, write_vectors,
        jnp.transpose(log_decay, (1, 0, 2)), segment_ids, out_grad,
    )


def fits(mesh, values):
    (layer_input, _, head_inputs, write_vectors, log_decay, _, _) = values
    return (
        mesh.shape["ctx"] == 1
        and mesh.shape["mdl"] == MDL
        and mesh.shape["dp"] == 2
        and layer_input.shape[:2] == (1, 2 * BLOCK_LEN)
        and log_decay.shape[1] == HEAD_N
        and head_inputs.shape[2] == HEAD_N * 64
        and write_vectors.shape[2] == 128
    )


def solution(mesh):
    def chosen(*values):
        if fits(mesh, values):
            return fused(*values)
        return per_device(*values)

    placed = (
        P(("grp", "dp"), "ctx", "mdl"),
        P("mdl", None),
        P(("grp", "dp"), "ctx", "mdl"),
        P(("grp", "dp"), "ctx", None),
        P(("grp", "dp"), "mdl", "ctx"),
        P(("grp", "dp"), "ctx"),
        P(("grp", "dp"), "ctx", "mdl"),
    )
    return jax.shard_map(
        chosen,
        mesh=mesh,
        in_specs=placed,
        out_specs=(P(("grp", "dp"), "ctx", "mdl"), P(("grp", "ctx", "dp"), "mdl")),
        check_vma=False,
    )
```

```python
import jax
import jax.numpy as jnp
from jax import lax
from jax.experimental import pallas as pl
from jax.experimental.pallas import tpu as pltpu
from jax.sharding import PartitionSpec as P

BLOCK_LEN = 512
MESH = pl.DeviceIdType.MESH
MDL = 8
SHARE = 2 * BLOCK_LEN // MDL
HALF = BLOCK_LEN // MDL
HEAD_N = 10
PAIRS = HEAD_N // 2
TILE = 256
LOG2E = 1.4426950408889634


def shifted(value, axis, by):
    count = lax.axis_size(axis)
    pairs = [(i, i + by) for i in range(count) if 0 <= i + by < count]
    return lax.ppermute(value, axis, pairs)


def join_parts(earlier, later):
    early_first, early_last, early_pass, leading_state = earlier
    later_first, later_last, later_pass, later_state = later
    linked = jnp.logical_or(
        early_last == later_first, jnp.logical_or(early_last < 0.0, later_first < 0.0)
    )
    carried = later_pass * linked.astype(jnp.float32)[..., None]
    front_seg = jnp.where(early_first < 0.0, later_first, early_first)
    back_seg = jnp.where(later_last < 0.0, early_last, later_last)
    return (
        front_seg,
        back_seg,
        early_pass * carried,
        later_state + carried[..., None, None] * leading_state,
    )


def per_device(
    layer_input, read_weight, head_inputs, write_vectors, log_decay, segment_ids, out_grad
):
    trace_count, length, model_cols = layer_input.shape
    head_count = log_decay.shape[1]
    head_dim = head_inputs.shape[2] // head_count
    state_dim = write_vectors.shape[2]
    block_count = length // BLOCK_LEN
    rows_all = trace_count * length
    flat_count = trace_count * block_count
    flat_input = layer_input.reshape(rows_all, model_cols)
    partial_value = jnp.dot(flat_input, read_weight, preferred_element_type=jnp.float32)
    readout = lax.psum(partial_value.astype(jnp.bfloat16), "mdl")
    segments = segment_ids.astype(jnp.float32).reshape(trace_count, block_count, BLOCK_LEN)
    decays = log_decay.reshape(trace_count, head_count, block_count, BLOCK_LEN)
    positions = jnp.arange(BLOCK_LEN)
    upper = (positions[:, None] <= positions[None, :]).astype(jnp.float32)
    cumulative = jnp.einsum("bhks,st->bhkt", decays, upper, precision=lax.Precision.HIGHEST)
    closing = cumulative[..., -1:]
    at_end = (segments == segments[..., -1:]).astype(jnp.float32)
    end_weight = jnp.exp(closing - cumulative) * at_end[:, None]
    values = head_inputs.reshape(trace_count, block_count, BLOCK_LEN, head_count, head_dim)
    keys_block = write_vectors.reshape(trace_count, block_count, BLOCK_LEN, state_dim)
    weighted = (values * jnp.transpose(end_weight, (0, 2, 3, 1))[..., None]).astype(jnp.bfloat16)
    block_states = jnp.einsum(
        "bkqhp,bkqn->kbhpn", weighted, keys_block, preferred_element_type=jnp.float32
    )
    front_seg = jnp.transpose(segments[..., 0])
    back_seg = jnp.transpose(segments[..., -1])
    single = (front_seg == back_seg).astype(jnp.float32)
    through = jnp.exp(jnp.transpose(closing[..., 0], (2, 0, 1))) * single[..., None]
    neutral = (
        -jnp.ones((trace_count,), jnp.float32),
        -jnp.ones((trace_count,), jnp.float32),
        jnp.ones((trace_count, head_count), jnp.float32),
        jnp.zeros((trace_count, head_count, head_dim, state_dim), jnp.float32),
    )

    def absorb(running, pieces):
        return (join_parts(running, pieces), running)

    device_total, prefixes = lax.scan(absorb, neutral, (front_seg, back_seg, through, block_states))
    position = lax.axis_index("ctx")

    def relay_once(iteration, incoming):
        outgoing = join_parts(incoming, device_total)
        shifted_lines = shifted((outgoing[0], outgoing[1], outgoing[2], outgoing[3]), "ctx", 1)
        return tuple(
            (
                jnp.where(position == 0, anchor, arrived)
                for anchor, arrived in zip(neutral, shifted_lines)
            )
        )

    entering = lax.fori_loop(0, lax.axis_size("ctx") - 1, relay_once, neutral)
    starts = join_parts(entering, prefixes)
    start_low = starts[3].astype(jnp.bfloat16)
    prior_seg = jnp.transpose(starts[1])
    coupled_items = (segments == prior_seg[..., None]).astype(jnp.float32)
    entry_gain = jnp.exp(cumulative) * coupled_items[:, None]
    gain_rows = jnp.transpose(entry_gain, (0, 2, 3, 1))[..., None]
    readout_block = readout.reshape(trace_count, block_count, BLOCK_LEN, state_dim)
    grads_block = out_grad.reshape(trace_count, block_count, BLOCK_LEN, head_count, head_dim)
    carried_out = (
        jnp.einsum(
            "bkqn,kbhpn->bkqhp", readout_block, start_low, preferred_element_type=jnp.float32
        )
        * gain_rows
    )
    per_head = jnp.einsum(
        "bkqhp,kbhpn->bkqhn", grads_block, start_low, preferred_element_type=jnp.float32
    )
    carried_back = jnp.sum(per_head * gain_rows, axis=3)
    causal = positions[:, None] >= positions[None, :]

    def inside(pieces):
        read_rows, key_rows, value_rows, grad_rows, cum_rows, seg_rows = pieces
        allowed = jnp.logical_and(causal, seg_rows[:, None] == seg_rows[None, :])
        spread = cum_rows[:, :, None] - cum_rows[:, None, :]
        weight = jnp.where(allowed[None], jnp.exp(jnp.where(allowed[None], spread, 0.0)), 0.0)
        scores = jnp.einsum("tn,sn->ts", read_rows, key_rows, preferred_element_type=jnp.float32)
        blend_factor = (weight * scores[None]).astype(jnp.bfloat16)
        inside_out = jnp.einsum(
            "hts,shp->thp", blend_factor, value_rows, preferred_element_type=jnp.float32
        )
        products = jnp.einsum(
            "thp,shp->hts", grad_rows, value_rows, preferred_element_type=jnp.float32
        )
        response = jnp.sum(weight * products, axis=0).astype(jnp.bfloat16)
        inside_back = jnp.dot(response, key_rows, preferred_element_type=jnp.float32)
        return (inside_out, inside_back)

    own_out, own_back = lax.map(
        inside,
        (
            readout_block.reshape(flat_count, BLOCK_LEN, state_dim),
            keys_block.reshape(flat_count, BLOCK_LEN, state_dim),
            values.reshape(flat_count, BLOCK_LEN, head_count, head_dim),
            grads_block.reshape(flat_count, BLOCK_LEN, head_count, head_dim),
            jnp.transpose(cumulative, (0, 2, 1, 3)).reshape(flat_count, head_count, BLOCK_LEN),
            segments.reshape(flat_count, BLOCK_LEN),
        ),
    )
    total_out = (
        own_out.reshape(trace_count, block_count, BLOCK_LEN, head_count, head_dim) + carried_out
    )
    head_outputs = total_out.astype(jnp.bfloat16).reshape(
        trace_count, length, head_count * head_dim
    )
    back_part = (
        own_back.reshape(trace_count, block_count, BLOCK_LEN, state_dim) + carried_back
    ).reshape(rows_all, state_dim)
    read_back = lax.psum(back_part.astype(jnp.bfloat16), "mdl")
    read_grad = lax.psum_scatter(
        lax.dot_general(
            read_back, flat_input, (((0,), (0,)), ((), ())), preferred_element_type=jnp.float32
        ),
        ("ctx", "dp"),
        scatter_dimension=0,
        tiled=True,
    )
    return (head_outputs, read_grad)


def fused_kernel(
    x_ref, w_ref, hi_hbm, wv_ref, ld_ref, seg_ref, og_hbm, out_hbm, grad_ref,
    hi_ref, og_ref, out_ref, kept,
    part, rs1, readout, back, rs2, rb, gfull, grecv,
    split, stack, rowx, colx, endx, entx, bias, resp, scores, start, carry,
    rs1_s, rs1_r, ag1_s, ag1_r, rs2_s, rs2_r, ag2_s, ag2_r, dp_s, dp_r, in_s, out_s,
):
    f32, bf16 = jnp.float32, jnp.bfloat16
    load_hi = pltpu.make_async_copy(hi_hbm, hi_ref, in_s.at[0])
    load_og = pltpu.make_async_copy(og_hbm, og_ref, in_s.at[1])
    load_hi.start()
    load_og.start()
    me = lax.axis_index("mdl")
    core = lax.axis_index("dp")
    peers = [lax.rem(me + o, MDL) for o in range(MDL)]
    barrier = pltpu.get_barrier_semaphore()
    for o in range(1, MDL):
        pl.semaphore_signal(barrier, inc=1, device_id={"mdl": peers[o]}, device_id_type=MESH)
    pl.semaphore_signal(barrier, inc=1, device_id={"dp": 1 - core}, device_id_type=MESH)

    def remote(src, dst, send, recv, to):
        copy = pltpu.make_async_remote_copy(
            src_ref=src, dst_ref=dst, send_sem=send, recv_sem=recv,
            device_id=to, device_id_type=MESH,
        )
        copy.start()
        return copy

    nn = (((1,), (1,)), ((), ()))
    tt = (((0,), (0,)), ((), ()))
    part[...] = lax.dot_general(x_ref[...], w_ref[...], tt, preferred_element_type=f32).astype(bf16)
    pl.semaphore_wait(barrier, MDL)
    first = [
        remote(
            part.at[pl.ds(pl.multiple_of(peers[o] * SHARE, SHARE), SHARE)], rs1.at[o],
            rs1_s.at[o], rs1_r.at[o], {"mdl": peers[o]},
        )
        for o in range(1, MDL)
    ]

    lane = lax.broadcasted_iota(jnp.int32, (1, 128), 1)
    left = lane < 64
    mask_a = left.astype(f32).astype(bf16)
    mask_b = (1.0 - left.astype(f32)).astype(bf16)
    rows_i = lax.broadcasted_iota(jnp.int32, (BLOCK_LEN, BLOCK_LEN), 0)
    cols_i = lax.broadcasted_iota(jnp.int32, (BLOCK_LEN, BLOCK_LEN), 1)
    upper = (rows_i <= cols_i).astype(f32).astype(bf16)

    def prepare(k):
        span = pl.ds(k * BLOCK_LEN, BLOCK_LEN)
        split[...] = jnp.zeros_like(split)
        stack[...] = jnp.zeros_like(stack)
        for h in range(HEAD_N):
            stack[pl.ds(h, 1), :] = ld_ref[h, :, span]
        rest = stack[pl.ds(0, 16), :]
        for piece in range(3):
            high = rest.astype(bf16).astype(f32)
            split[pl.ds(16 * piece, 16), :] = high
            rest = rest - high
        sums = jnp.dot(split[...].astype(bf16), upper, preferred_element_type=f32)
        cum = (sums[0:16] + sums[16:32] + sums[32:48]) * LOG2E
        seg = seg_ref[:, span].astype(f32)
        stack[pl.ds(0, 16), :] = cum
        if k == 0:
            close = cum[:, BLOCK_LEN - 1 :]
            at_end = (seg == seg[:, BLOCK_LEN - 1 :]).astype(f32)
            stack[pl.ds(16, 16), :] = jnp.exp2(close - cum) * at_end
        else:
            prior = seg_ref[:, pl.ds(BLOCK_LEN - 128, 128)].astype(f32)[:, 127:]
            stack[pl.ds(32, 16), :] = jnp.exp2(cum) * (seg == prior).astype(f32)
        stack[pl.ds(48, 8), :] = jnp.broadcast_to(seg, (8, BLOCK_LEN))
        turned = stack[...].T
        for h in range(HEAD_N):
            rowx[k, h] = cum[h : h + 1, :]
            colx[k, h] = jnp.broadcast_to(turned[:, h : h + 1], (BLOCK_LEN, 128))
        for j in range(PAIRS):
            base, target = (16, endx) if k == 0 else (32, entx)
            a = turned[:, base + 2 * j : base + 2 * j + 1]
            b = turned[:, base + 2 * j + 1 : base + 2 * j + 2]
            target[j] = jnp.where(left, a, b)
        same = jnp.logical_and(turned[:, 48:49] == seg, rows_i >= cols_i)
        bias[k] = jnp.where(same, 0.0, -1e30)

    def weight(k, h, i, wide):
        rows = pl.ds(i * TILE, TILE)
        col = colx[k, h, rows, :]
        col = jnp.concatenate([col] * (wide // 128), axis=1)
        return jnp.exp2((col - rowx[k, h, :, pl.ds(0, wide)]) + bias[k, rows, pl.ds(0, wide)])

    def lanes_of(j):
        return pl.ds(pl.multiple_of(j * 128, 128), 128)

    def backward(k):
        resp[...] = jnp.zeros_like(resp)
        carry[...] = jnp.zeros_like(carry)
        keys = wv_ref[0, pl.ds(k * BLOCK_LEN, BLOCK_LEN), :]

        def body(j, _):
            lanes = lanes_of(j)
            if k == 0:
                value = hi_ref[0, pl.ds(0, BLOCK_LEN), lanes].astype(f32)
                low = (value * endx[j]).astype(bf16)
                start[j] = lax.dot_general(low, keys, tt, preferred_element_type=f32).astype(bf16)
            else:
                grads = og_ref[0, pl.ds(BLOCK_LEN, BLOCK_LEN), lanes].astype(f32)
                carry[...] += jnp.dot(
                    (grads * entx[j]).astype(bf16), start[j], preferred_element_type=f32
                )
            for i in range(BLOCK_LEN // TILE):
                wide = (i + 1) * TILE
                value = hi_ref[0, pl.ds(k * BLOCK_LEN, wide), lanes]
                grads = og_ref[0, pl.ds(k * BLOCK_LEN + i * TILE, TILE), lanes]
                pa = lax.dot_general(grads * mask_a, value, nn, preferred_element_type=f32)
                pb = lax.dot_general(grads * mask_b, value, nn, preferred_element_type=f32)
                wa = weight(k, 2 * j, i, wide)
                wb = weight(k, 2 * j + 1, i, wide)
                rows = pl.ds(i * TILE, TILE)
                kept[k, 2 * j, rows, pl.ds(0, wide)] = wa.astype(bf16)
                kept[k, 2 * j + 1, rows, pl.ds(0, wide)] = wb.astype(bf16)
                resp[rows, pl.ds(0, wide)] += wa * pa + wb * pb
            return 0

        lax.fori_loop(0, PAIRS, body, 0)
        total = jnp.dot(resp[...].astype(bf16), keys, preferred_element_type=f32) + carry[...]
        back[pl.ds(k * BLOCK_LEN, BLOCK_LEN), :] = total.astype(bf16)
        return [
            remote(
                back.at[pl.ds(pl.multiple_of(k * BLOCK_LEN + peers[o] * HALF, HALF), HALF)],
                rs2.at[k, o], rs2_s.at[k, o], rs2_r.at[k, o], {"mdl": peers[o]},
            )
            for o in range(1, MDL)
        ]

    def forward(k):
        keys = wv_ref[0, pl.ds(k * BLOCK_LEN, BLOCK_LEN), :]
        reads = readout[pl.ds(k * BLOCK_LEN, BLOCK_LEN), :]
        scores[...] = lax.dot_general(reads, keys, nn, preferred_element_type=f32).astype(bf16)

        def body(j, _):
            lanes = lanes_of(j)
            for i in range(BLOCK_LEN // TILE):
                wide = (i + 1) * TILE
                value = hi_ref[0, pl.ds(k * BLOCK_LEN, wide), lanes]
                rows = pl.ds(i * TILE, TILE)
                score = scores[rows, pl.ds(0, wide)]
                mix_a = kept[k, 2 * j, rows, pl.ds(0, wide)] * score
                mix_b = kept[k, 2 * j + 1, rows, pl.ds(0, wide)] * score
                oa = jnp.dot(mix_a, value, preferred_element_type=f32)
                ob = jnp.dot(mix_b, value, preferred_element_type=f32)
                total = jnp.where(left, oa, ob)
                if k == 1:
                    carried = lax.dot_general(
                        readout[pl.ds(BLOCK_LEN + i * TILE, TILE), :], start[j], nn,
                        preferred_element_type=f32,
                    )
                    total = total + carried * entx[j, pl.ds(i * TILE, TILE), :]
                out_ref[0, pl.ds(k * BLOCK_LEN + i * TILE, TILE), lanes] = total.astype(bf16)
            return 0

        lax.fori_loop(0, PAIRS, body, 0)
        span = pl.ds(k * BLOCK_LEN, BLOCK_LEN)
        store = pltpu.make_async_copy(out_ref.at[:, span], out_hbm.at[:, span], out_s.at[k])
        store.start()
        return store

    across = me + 1 - 2 * lax.rem(me, 2)
    lines = [lax.rem(me + 2 * q, MDL) for q in range(4)]
    origins = [lax.rem(me + MDL - 2 * q, MDL) for q in range(4)]

    def gather(ref, begin, size, send, recv):
        mine = pl.ds(pl.multiple_of(begin + me * size, size), size)
        near = [
            remote(ref.at[mine], ref.at[mine], send(q), recv(q), {"mdl": lines[q]})
            for q in (2, 3, 1)
        ]
        return near, [remote(ref.at[mine], ref.at[mine], send(4), recv(4), {"mdl": across})]

    def relay(copies, ref, begin, size, send, recv):
        near, far = copies
        for at in (2, 1, 0):
            q = (2, 3, 1)[at]
            near[at].wait_recv()
            rows = pl.ds(pl.multiple_of(begin + origins[q] * size, size), size)
            far.append(
                remote(ref.at[rows], ref.at[rows], send(4 + q), recv(4 + q), {"mdl": across})
            )
        return near + far, far

    sems_1 = (lambda o: ag1_s.at[o]), (lambda o: ag1_r.at[o])
    sems_2 = [
        ((lambda o: ag2_s.at[0, o]), (lambda o: ag2_r.at[0, o])),
    ]

    def collect(k, copies):
        mine = pl.ds(pl.multiple_of(k * BLOCK_LEN + me * HALF, HALF), HALF)
        total = back[mine, :].astype(f32)
        for o in range(1, MDL):
            copies[o - 1].wait_recv()
            total = total + rs2[k, o].astype(f32)
        rb[mine, :] = total.astype(bf16)
        if k == 0:
            return gather(rb, 0, HALF, *sems_2[0])
        return [
            remote(rb.at[mine], rb.at[mine], ag2_s.at[1, o], ag2_r.at[1, o], {"mdl": peers[o]})
            for o in range(1, MDL)
        ]

    prepare(0)
    load_hi.wait()
    load_og.wait()
    back_0 = backward(0)
    mine = pl.ds(pl.multiple_of(me * SHARE, SHARE), SHARE)
    total = part[mine, :].astype(f32)
    for o in range(1, MDL):
        first[o - 1].wait_recv()
        total = total + rs1[o].astype(f32)
    readout[mine, :] = total.astype(bf16)
    spread = gather(readout, 0, SHARE, *sems_1)
    prepare(1)
    back_1 = backward(1)
    spread, landing = relay(spread, readout, 0, SHARE, *sems_1)
    gather_0 = collect(0, back_0)
    for copy in landing:
        copy.wait_recv()
    store_0 = forward(0)
    gather_1 = collect(1, back_1)
    gather_0, landing_0 = relay(gather_0, rb, 0, HALF, *sems_2[0])
    store_1 = forward(1)
    for copy in landing_0:
        copy.wait_recv()
    turn = (((0,), (1,)), ((), ()))
    halves = [pl.ds(0, BLOCK_LEN), pl.ds(BLOCK_LEN, BLOCK_LEN)]
    gfull[...] = lax.dot_general(
        rb[halves[0], :], x_ref[:, halves[0]], turn, preferred_element_type=f32
    )
    for copy in gather_1:
        copy.wait_recv()
    gfull[...] += lax.dot_general(
        rb[halves[1], :], x_ref[:, halves[1]], turn, preferred_element_type=f32
    )
    owner = 1 - core
    swap = remote(
        gfull.at[pl.ds(pl.multiple_of(owner * 64, 64), 64)], grecv, dp_s, dp_r, {"dp": owner}
    )
    swap.wait_recv()
    grad_ref[...] = gfull[pl.ds(pl.multiple_of(core * 64, 64), 64), :] + grecv[...]
    swap.wait_send()
    store_0.wait()
    store_1.wait()
    for copy in first + spread + back_0 + back_1 + gather_0 + gather_1:
        copy.wait_send()


def fused(layer_input, read_weight, head_inputs, write_vectors, log_decay, segment_ids, out_grad):
    f32, bf16 = jnp.float32, jnp.bfloat16
    dma = pltpu.SemaphoreType.DMA
    vmem = pl.BlockSpec(memory_space=pltpu.VMEM)
    anywhere = pl.BlockSpec(memory_space=pl.ANY)
    length = layer_input.shape[1]
    cols = layer_input.shape[2]
    state = write_vectors.shape[2]
    square = (BLOCK_LEN, BLOCK_LEN)
    return pl.pallas_call(
        fused_kernel,
        out_shape=(
            jax.ShapeDtypeStruct(head_inputs.shape, bf16),
            jax.ShapeDtypeStruct((state // 2, cols), f32),
        ),
        in_specs=[vmem, vmem, anywhere, vmem, vmem, vmem, anywhere],
        out_specs=(anywhere, vmem),
        scratch_shapes=[
            pltpu.VMEM(head_inputs.shape, bf16),
            pltpu.VMEM(head_inputs.shape, bf16),
            pltpu.VMEM(head_inputs.shape, bf16),
            pltpu.VMEM((2, HEAD_N) + square, bf16),
            pltpu.VMEM((length, state), bf16),
            pltpu.VMEM((MDL, SHARE, state), bf16),
            pltpu.VMEM((length, state), bf16),
            pltpu.VMEM((length, state), bf16),
            pltpu.VMEM((2, MDL, HALF, state), bf16),
            pltpu.VMEM((length, state), bf16),
            pltpu.VMEM((state, cols), f32),
            pltpu.VMEM((state // 2, cols), f32),
            pltpu.VMEM((48, BLOCK_LEN), f32),
            pltpu.VMEM((128, BLOCK_LEN), f32),
            pltpu.VMEM((2, HEAD_N, 1, BLOCK_LEN), f32),
            pltpu.VMEM((2, HEAD_N, BLOCK_LEN, 128), f32),
            pltpu.VMEM((PAIRS, BLOCK_LEN, 128), f32),
            pltpu.VMEM((PAIRS, BLOCK_LEN, 128), f32),
            pltpu.VMEM((2,) + square, f32),
            pltpu.VMEM(square, f32),
            pltpu.VMEM(square, bf16),
            pltpu.VMEM((PAIRS, 128, state), bf16),
            pltpu.VMEM((BLOCK_LEN, state), f32),
            dma((MDL,)), dma((MDL,)), dma((MDL,)), dma((MDL,)),
            dma((2, MDL)), dma((2, MDL)), dma((2, MDL)), dma((2, MDL)),
            dma, dma, dma((2,)), dma((2,)),
        ],
        compiler_params=pltpu.CompilerParams(
            collective_id=0, has_side_effects=True, vmem_limit_bytes=56 * 1024 * 1024
        ),
    )(
        layer_input.reshape(length, cols).T, read_weight, head_inputs, write_vectors,
        jnp.transpose(log_decay, (1, 0, 2)), segment_ids, out_grad,
    )


def fits(mesh, values):
    (layer_input, _, head_inputs, write_vectors, log_decay, _, _) = values
    return (
        mesh.shape["ctx"] == 1
        and mesh.shape["mdl"] == MDL
        and mesh.shape["dp"] == 2
        and layer_input.shape[:2] == (1, 2 * BLOCK_LEN)
        and log_decay.shape[1] == HEAD_N
        and head_inputs.shape[2] == HEAD_N * 64
        and write_vectors.shape[2] == 128
    )


def solution(mesh):
    def chosen(*values):
        if fits(mesh, values):
            return fused(*values)
        return per_device(*values)

    placed = (
        P(("grp", "dp"), "ctx", "mdl"),
        P("mdl", None),
        P(("grp", "dp"), "ctx", "mdl"),
        P(("grp", "dp"), "ctx", None),
        P(("grp", "dp"), "mdl", "ctx"),
        P(("grp", "dp"), "ctx"),
        P(("grp", "dp"), "ctx", "mdl"),
    )
    return jax.shard_map(
        chosen,
        mesh=mesh,
        in_specs=placed,
        out_specs=(P(("grp", "dp"), "ctx", "mdl"), P(("grp", "ctx", "dp"), "mdl")),
        check_vma=False,
    )
```

```python
import jax
import jax.numpy as jnp
from jax import lax
from jax.experimental import pallas as pl
from jax.experimental.pallas import tpu as pltpu
from jax.sharding import PartitionSpec as P

BLOCK_LEN = 512
MESH = pl.DeviceIdType.MESH
MDL = 8
SHARE = 2 * BLOCK_LEN // MDL
HALF = BLOCK_LEN // MDL
HEAD_N = 10
PAIRS = HEAD_N // 2
TILE = 256
LOG2E = 1.4426950408889634


def shifted(value, axis, by):
    count = lax.axis_size(axis)
    pairs = [(i, i + by) for i in range(count) if 0 <= i + by < count]
    return lax.ppermute(value, axis, pairs)


def join_parts(earlier, later):
    early_first, early_last, early_pass, leading_state = earlier
    later_first, later_last, later_pass, later_state = later
    linked = jnp.logical_or(
        early_last == later_first, jnp.logical_or(early_last < 0.0, later_first < 0.0)
    )
    carried = later_pass * linked.astype(jnp.float32)[..., None]
    front_seg = jnp.where(early_first < 0.0, later_first, early_first)
    back_seg = jnp.where(later_last < 0.0, early_last, later_last)
    return (
        front_seg,
        back_seg,
        early_pass * carried,
        later_state + carried[..., None, None] * leading_state,
    )


def per_device(
    layer_input, read_weight, head_inputs, write_vectors, log_decay, segment_ids, out_grad
):
    trace_count, length, model_cols = layer_input.shape
    head_count = log_decay.shape[1]
    head_dim = head_inputs.shape[2] // head_count
    state_dim = write_vectors.shape[2]
    block_count = length // BLOCK_LEN
    rows_all = trace_count * length
    flat_count = trace_count * block_count
    flat_input = layer_input.reshape(rows_all, model_cols)
    partial_value = jnp.dot(flat_input, read_weight, preferred_element_type=jnp.float32)
    readout = lax.psum(partial_value.astype(jnp.bfloat16), "mdl")
    segments = segment_ids.astype(jnp.float32).reshape(trace_count, block_count, BLOCK_LEN)
    decays = log_decay.reshape(trace_count, head_count, block_count, BLOCK_LEN)
    positions = jnp.arange(BLOCK_LEN)
    upper = (positions[:, None] <= positions[None, :]).astype(jnp.float32)
    cumulative = jnp.einsum("bhks,st->bhkt", decays, upper, precision=lax.Precision.HIGHEST)
    closing = cumulative[..., -1:]
    at_end = (segments == segments[..., -1:]).astype(jnp.float32)
    end_weight = jnp.exp(closing - cumulative) * at_end[:, None]
    values = head_inputs.reshape(trace_count, block_count, BLOCK_LEN, head_count, head_dim)
    keys_block = write_vectors.reshape(trace_count, block_count, BLOCK_LEN, state_dim)
    weighted = (values * jnp.transpose(end_weight, (0, 2, 3, 1))[..., None]).astype(jnp.bfloat16)
    block_states = jnp.einsum(
        "bkqhp,bkqn->kbhpn", weighted, keys_block, preferred_element_type=jnp.float32
    )
    front_seg = jnp.transpose(segments[..., 0])
    back_seg = jnp.transpose(segments[..., -1])
    single = (front_seg == back_seg).astype(jnp.float32)
    through = jnp.exp(jnp.transpose(closing[..., 0], (2, 0, 1))) * single[..., None]
    neutral = (
        -jnp.ones((trace_count,), jnp.float32),
        -jnp.ones((trace_count,), jnp.float32),
        jnp.ones((trace_count, head_count), jnp.float32),
        jnp.zeros((trace_count, head_count, head_dim, state_dim), jnp.float32),
    )

    def absorb(running, pieces):
        return (join_parts(running, pieces), running)

    device_total, prefixes = lax.scan(absorb, neutral, (front_seg, back_seg, through, block_states))
    position = lax.axis_index("ctx")

    def relay_once(iteration, incoming):
        outgoing = join_parts(incoming, device_total)
        shifted_lines = shifted((outgoing[0], outgoing[1], outgoing[2], outgoing[3]), "ctx", 1)
        return tuple(
            (
                jnp.where(position == 0, anchor, arrived)
                for anchor, arrived in zip(neutral, shifted_lines)
            )
        )

    entering = lax.fori_loop(0, lax.axis_size("ctx") - 1, relay_once, neutral)
    starts = join_parts(entering, prefixes)
    start_low = starts[3].astype(jnp.bfloat16)
    prior_seg = jnp.transpose(starts[1])
    coupled_items = (segments == prior_seg[..., None]).astype(jnp.float32)
    entry_gain = jnp.exp(cumulative) * coupled_items[:, None]
    gain_rows = jnp.transpose(entry_gain, (0, 2, 3, 1))[..., None]
    readout_block = readout.reshape(trace_count, block_count, BLOCK_LEN, state_dim)
    grads_block = out_grad.reshape(trace_count, block_count, BLOCK_LEN, head_count, head_dim)
    carried_out = (
        jnp.einsum(
            "bkqn,kbhpn->bkqhp", readout_block, start_low, preferred_element_type=jnp.float32
        )
        * gain_rows
    )
    per_head = jnp.einsum(
        "bkqhp,kbhpn->bkqhn", grads_block, start_low, preferred_element_type=jnp.float32
    )
    carried_back = jnp.sum(per_head * gain_rows, axis=3)
    causal = positions[:, None] >= positions[None, :]

    def inside(pieces):
        read_rows, key_rows, value_rows, grad_rows, cum_rows, seg_rows = pieces
        allowed = jnp.logical_and(causal, seg_rows[:, None] == seg_rows[None, :])
        spread = cum_rows[:, :, None] - cum_rows[:, None, :]
        weight = jnp.where(allowed[None], jnp.exp(jnp.where(allowed[None], spread, 0.0)), 0.0)
        scores = jnp.einsum("tn,sn->ts", read_rows, key_rows, preferred_element_type=jnp.float32)
        blend_factor = (weight * scores[None]).astype(jnp.bfloat16)
        inside_out = jnp.einsum(
            "hts,shp->thp", blend_factor, value_rows, preferred_element_type=jnp.float32
        )
        products = jnp.einsum(
            "thp,shp->hts", grad_rows, value_rows, preferred_element_type=jnp.float32
        )
        response = jnp.sum(weight * products, axis=0).astype(jnp.bfloat16)
        inside_back = jnp.dot(response, key_rows, preferred_element_type=jnp.float32)
        return (inside_out, inside_back)

    own_out, own_back = lax.map(
        inside,
        (
            readout_block.reshape(flat_count, BLOCK_LEN, state_dim),
            keys_block.reshape(flat_count, BLOCK_LEN, state_dim),
            values.reshape(flat_count, BLOCK_LEN, head_count, head_dim),
            grads_block.reshape(flat_count, BLOCK_LEN, head_count, head_dim),
            jnp.transpose(cumulative, (0, 2, 1, 3)).reshape(flat_count, head_count, BLOCK_LEN),
            segments.reshape(flat_count, BLOCK_LEN),
        ),
    )
    total_out = (
        own_out.reshape(trace_count, block_count, BLOCK_LEN, head_count, head_dim) + carried_out
    )
    head_outputs = total_out.astype(jnp.bfloat16).reshape(
        trace_count, length, head_count * head_dim
    )
    back_part = (
        own_back.reshape(trace_count, block_count, BLOCK_LEN, state_dim) + carried_back
    ).reshape(rows_all, state_dim)
    read_back = lax.psum(back_part.astype(jnp.bfloat16), "mdl")
    read_grad = lax.psum_scatter(
        lax.dot_general(
            read_back, flat_input, (((0,), (0,)), ((), ())), preferred_element_type=jnp.float32
        ),
        ("ctx", "dp"),
        scatter_dimension=0,
        tiled=True,
    )
    return (head_outputs, read_grad)


def fused_kernel(
    x_ref, w_ref, hi_hbm, wv_ref, ld_ref, seg_ref, og_hbm, out_hbm, grad_ref,
    hi_ref, og_ref, out_ref, kept,
    part, rs1, readout, back, rs2, rb, gfull, grecv,
    split, stack, rowx, colx, endx, entx, bias, resp, scores, start, carry,
    rs1_s, rs1_r, ag1_s, ag1_r, rs2_s, rs2_r, ag2_s, ag2_r, dp_s, dp_r, in_s, out_s,
):
    f32, bf16 = jnp.float32, jnp.bfloat16
    load_hi = pltpu.make_async_copy(hi_hbm, hi_ref, in_s.at[0])
    load_og = pltpu.make_async_copy(og_hbm, og_ref, in_s.at[1])
    load_hi.start()
    load_og.start()
    me = lax.axis_index("mdl")
    core = lax.axis_index("dp")
    peers = [lax.rem(me + o, MDL) for o in range(MDL)]
    barrier = pltpu.get_barrier_semaphore()
    for o in range(1, MDL):
        pl.semaphore_signal(barrier, inc=1, device_id={"mdl": peers[o]}, device_id_type=MESH)
    pl.semaphore_signal(barrier, inc=1, device_id={"dp": 1 - core}, device_id_type=MESH)

    def remote(src, dst, send, recv, to):
        copy = pltpu.make_async_remote_copy(
            src_ref=src, dst_ref=dst, send_sem=send, recv_sem=recv,
            device_id=to, device_id_type=MESH,
        )
        copy.start()
        return copy

    nn = (((1,), (1,)), ((), ()))
    tt = (((0,), (0,)), ((), ()))
    part[...] = lax.dot_general(x_ref[...], w_ref[...], tt, preferred_element_type=f32).astype(bf16)
    pl.semaphore_wait(barrier, MDL)
    first = [
        remote(
            part.at[pl.ds(pl.multiple_of(peers[o] * SHARE, SHARE), SHARE)], rs1.at[o],
            rs1_s.at[o], rs1_r.at[o], {"mdl": peers[o]},
        )
        for o in range(1, MDL)
    ]

    lane = lax.broadcasted_iota(jnp.int32, (1, 128), 1)
    left = lane < 64
    mask_a = left.astype(f32).astype(bf16)
    mask_b = (1.0 - left.astype(f32)).astype(bf16)
    rows_i = lax.broadcasted_iota(jnp.int32, (BLOCK_LEN, BLOCK_LEN), 0)
    cols_i = lax.broadcasted_iota(jnp.int32, (BLOCK_LEN, BLOCK_LEN), 1)
    upper = (rows_i <= cols_i).astype(f32).astype(bf16)

    def prepare(k):
        span = pl.ds(k * BLOCK_LEN, BLOCK_LEN)
        split[...] = jnp.zeros_like(split)
        stack[...] = jnp.zeros_like(stack)
        for h in range(HEAD_N):
            stack[pl.ds(h, 1), :] = ld_ref[h, :, span]
        rest = stack[pl.ds(0, 16), :]
        for piece in range(3):
            high = rest.astype(bf16).astype(f32)
            split[pl.ds(16 * piece, 16), :] = high
            rest = rest - high
        sums = jnp.dot(split[...].astype(bf16), upper, preferred_element_type=f32)
        cum = (sums[0:16] + sums[16:32] + sums[32:48]) * LOG2E
        seg = seg_ref[:, span].astype(f32)
        stack[pl.ds(0, 16), :] = cum
        if k == 0:
            close = cum[:, BLOCK_LEN - 1 :]
            at_end = (seg == seg[:, BLOCK_LEN - 1 :]).astype(f32)
            stack[pl.ds(16, 16), :] = jnp.exp2(close - cum) * at_end
        else:
            prior = seg_ref[:, pl.ds(BLOCK_LEN - 128, 128)].astype(f32)[:, 127:]
            stack[pl.ds(32, 16), :] = jnp.exp2(cum) * (seg == prior).astype(f32)
        stack[pl.ds(48, 8), :] = jnp.broadcast_to(seg, (8, BLOCK_LEN))
        turned = stack[...].T
        for h in range(HEAD_N):
            rowx[k, h] = cum[h : h + 1, :]
            colx[k, h] = jnp.broadcast_to(turned[:, h : h + 1], (BLOCK_LEN, 128))
        for j in range(PAIRS):
            base, target = (16, endx) if k == 0 else (32, entx)
            a = turned[:, base + 2 * j : base + 2 * j + 1]
            b = turned[:, base + 2 * j + 1 : base + 2 * j + 2]
            target[j] = jnp.where(left, a, b)
        same = jnp.logical_and(turned[:, 48:49] == seg, rows_i >= cols_i)
        bias[k] = jnp.where(same, 0.0, -1e30)

    def weight(k, h, i, wide):
        rows = pl.ds(i * TILE, TILE)
        col = colx[k, h, rows, :]
        col = jnp.concatenate([col] * (wide // 128), axis=1)
        return jnp.exp2((col - rowx[k, h, :, pl.ds(0, wide)]) + bias[k, rows, pl.ds(0, wide)])

    def lanes_of(j):
        return pl.ds(pl.multiple_of(j * 128, 128), 128)

    def backward(k, between=None):
        resp[...] = jnp.zeros_like(resp)
        carry[...] = jnp.zeros_like(carry)
        keys = wv_ref[0, pl.ds(k * BLOCK_LEN, BLOCK_LEN), :]

        def body(j, _):
            lanes = lanes_of(j)
            if k == 0:
                value = hi_ref[0, pl.ds(0, BLOCK_LEN), lanes].astype(f32)
                low = (value * endx[j]).astype(bf16)
                start[j] = lax.dot_general(low, keys, tt, preferred_element_type=f32).astype(bf16)
            else:
                grads = og_ref[0, pl.ds(BLOCK_LEN, BLOCK_LEN), lanes].astype(f32)
                carry[...] += jnp.dot(
                    (grads * entx[j]).astype(bf16), start[j], preferred_element_type=f32
                )
            for i in range(BLOCK_LEN // TILE):
                wide = (i + 1) * TILE
                value = hi_ref[0, pl.ds(k * BLOCK_LEN, wide), lanes]
                grads = og_ref[0, pl.ds(k * BLOCK_LEN + i * TILE, TILE), lanes]
                pa = lax.dot_general(grads * mask_a, value, nn, preferred_element_type=f32)
                pb = lax.dot_general(grads * mask_b, value, nn, preferred_element_type=f32)
                wa = weight(k, 2 * j, i, wide)
                wb = weight(k, 2 * j + 1, i, wide)
                rows = pl.ds(i * TILE, TILE)
                kept[k, 2 * j, rows, pl.ds(0, wide)] = wa.astype(bf16)
                kept[k, 2 * j + 1, rows, pl.ds(0, wide)] = wb.astype(bf16)
                resp[rows, pl.ds(0, wide)] += wa * pa + wb * pb
            return 0

        issued = None
        if between is None:
            lax.fori_loop(0, PAIRS, body, 0)
        else:
            lax.fori_loop(0, 3, body, 0)
            issued = between()
            lax.fori_loop(3, PAIRS, body, 0)
        total = jnp.dot(resp[...].astype(bf16), keys, preferred_element_type=f32) + carry[...]
        back[pl.ds(k * BLOCK_LEN, BLOCK_LEN), :] = total.astype(bf16)
        sent = [
            remote(
                back.at[pl.ds(pl.multiple_of(k * BLOCK_LEN + peers[o] * HALF, HALF), HALF)],
                rs2.at[k, o], rs2_s.at[k, o], rs2_r.at[k, o], {"mdl": peers[o]},
            )
            for o in range(1, MDL)
        ]
        return sent, issued

    def forward(k):
        keys = wv_ref[0, pl.ds(k * BLOCK_LEN, BLOCK_LEN), :]
        reads = readout[pl.ds(k * BLOCK_LEN, BLOCK_LEN), :]
        scores[...] = lax.dot_general(reads, keys, nn, preferred_element_type=f32).astype(bf16)

        def body(j, _):
            lanes = lanes_of(j)
            for i in range(BLOCK_LEN // TILE):
                wide = (i + 1) * TILE
                value = hi_ref[0, pl.ds(k * BLOCK_LEN, wide), lanes]
                rows = pl.ds(i * TILE, TILE)
                score = scores[rows, pl.ds(0, wide)]
                mix_a = kept[k, 2 * j, rows, pl.ds(0, wide)] * score
                mix_b = kept[k, 2 * j + 1, rows, pl.ds(0, wide)] * score
                oa = jnp.dot(mix_a, value, preferred_element_type=f32)
                ob = jnp.dot(mix_b, value, preferred_element_type=f32)
                total = jnp.where(left, oa, ob)
                if k == 1:
                    carried = lax.dot_general(
                        readout[pl.ds(BLOCK_LEN + i * TILE, TILE), :], start[j], nn,
                        preferred_element_type=f32,
                    )
                    total = total + carried * entx[j, pl.ds(i * TILE, TILE), :]
                out_ref[0, pl.ds(k * BLOCK_LEN + i * TILE, TILE), lanes] = total.astype(bf16)
            return 0

        lax.fori_loop(0, PAIRS, body, 0)
        span = pl.ds(k * BLOCK_LEN, BLOCK_LEN)
        store = pltpu.make_async_copy(out_ref.at[:, span], out_hbm.at[:, span], out_s.at[k])
        store.start()
        return store

    across = me + 1 - 2 * lax.rem(me, 2)
    lines = [lax.rem(me + 2 * q, MDL) for q in range(4)]
    origins = [lax.rem(me + MDL - 2 * q, MDL) for q in range(4)]

    def gather(ref, begin, size, send, recv):
        mine = pl.ds(pl.multiple_of(begin + me * size, size), size)
        near = [
            remote(ref.at[mine], ref.at[mine], send(q), recv(q), {"mdl": lines[q]})
            for q in (2, 3, 1)
        ]
        return near, [remote(ref.at[mine], ref.at[mine], send(4), recv(4), {"mdl": across})]

    def relay(copies, ref, begin, size, send, recv):
        near, far = copies
        for at in (2, 1, 0):
            q = (2, 3, 1)[at]
            near[at].wait_recv()
            rows = pl.ds(pl.multiple_of(begin + origins[q] * size, size), size)
            far.append(
                remote(ref.at[rows], ref.at[rows], send(4 + q), recv(4 + q), {"mdl": across})
            )
        return near + far, far

    sems_1 = (lambda o: ag1_s.at[o]), (lambda o: ag1_r.at[o])
    sems_2 = [
        ((lambda o: ag2_s.at[0, o]), (lambda o: ag2_r.at[0, o])),
    ]

    def collect(k, copies):
        mine = pl.ds(pl.multiple_of(k * BLOCK_LEN + me * HALF, HALF), HALF)
        total = back[mine, :].astype(f32)
        for o in range(1, MDL):
            copies[o - 1].wait_recv()
            total = total + rs2[k, o].astype(f32)
        rb[mine, :] = total.astype(bf16)
        if k == 0:
            return gather(rb, 0, HALF, *sems_2[0])
        return [
            remote(rb.at[mine], rb.at[mine], ag2_s.at[1, o], ag2_r.at[1, o], {"mdl": peers[o]})
            for o in range(1, MDL)
        ]

    prepare(0)
    load_hi.wait()
    load_og.wait()
    back_0, _ = backward(0)
    mine = pl.ds(pl.multiple_of(me * SHARE, SHARE), SHARE)
    total = part[mine, :].astype(f32)
    for o in range(1, MDL):
        first[o - 1].wait_recv()
        total = total + rs1[o].astype(f32)
    readout[mine, :] = total.astype(bf16)
    begun = gather(readout, 0, SHARE, *sems_1)
    prepare(1)

    def between():
        return relay(begun, readout, 0, SHARE, *sems_1), collect(0, back_0)

    back_1, ((spread, landing), gather_0) = backward(1, between)
    for copy in landing:
        copy.wait_recv()
    store_0 = forward(0)
    gather_1 = collect(1, back_1)
    gather_0, landing_0 = relay(gather_0, rb, 0, HALF, *sems_2[0])
    store_1 = forward(1)
    for copy in landing_0:
        copy.wait_recv()
    turn = (((0,), (1,)), ((), ()))
    halves = [pl.ds(0, BLOCK_LEN), pl.ds(BLOCK_LEN, BLOCK_LEN)]
    gfull[...] = lax.dot_general(
        rb[halves[0], :], x_ref[:, halves[0]], turn, preferred_element_type=f32
    )
    for copy in gather_1:
        copy.wait_recv()
    gfull[...] += lax.dot_general(
        rb[halves[1], :], x_ref[:, halves[1]], turn, preferred_element_type=f32
    )
    owner = 1 - core
    swap = remote(
        gfull.at[pl.ds(pl.multiple_of(owner * 64, 64), 64)], grecv, dp_s, dp_r, {"dp": owner}
    )
    swap.wait_recv()
    grad_ref[...] = gfull[pl.ds(pl.multiple_of(core * 64, 64), 64), :] + grecv[...]
    swap.wait_send()
    store_0.wait()
    store_1.wait()
    for copy in first + spread + back_0 + back_1 + gather_0 + gather_1:
        copy.wait_send()


def fused(layer_input, read_weight, head_inputs, write_vectors, log_decay, segment_ids, out_grad):
    f32, bf16 = jnp.float32, jnp.bfloat16
    dma = pltpu.SemaphoreType.DMA
    vmem = pl.BlockSpec(memory_space=pltpu.VMEM)
    anywhere = pl.BlockSpec(memory_space=pl.ANY)
    length = layer_input.shape[1]
    cols = layer_input.shape[2]
    state = write_vectors.shape[2]
    square = (BLOCK_LEN, BLOCK_LEN)
    return pl.pallas_call(
        fused_kernel,
        out_shape=(
            jax.ShapeDtypeStruct(head_inputs.shape, bf16),
            jax.ShapeDtypeStruct((state // 2, cols), f32),
        ),
        in_specs=[vmem, vmem, anywhere, vmem, vmem, vmem, anywhere],
        out_specs=(anywhere, vmem),
        scratch_shapes=[
            pltpu.VMEM(head_inputs.shape, bf16),
            pltpu.VMEM(head_inputs.shape, bf16),
            pltpu.VMEM(head_inputs.shape, bf16),
            pltpu.VMEM((2, HEAD_N) + square, bf16),
            pltpu.VMEM((length, state), bf16),
            pltpu.VMEM((MDL, SHARE, state), bf16),
            pltpu.VMEM((length, state), bf16),
            pltpu.VMEM((length, state), bf16),
            pltpu.VMEM((2, MDL, HALF, state), bf16),
            pltpu.VMEM((length, state), bf16),
            pltpu.VMEM((state, cols), f32),
            pltpu.VMEM((state // 2, cols), f32),
            pltpu.VMEM((48, BLOCK_LEN), f32),
            pltpu.VMEM((128, BLOCK_LEN), f32),
            pltpu.VMEM((2, HEAD_N, 1, BLOCK_LEN), f32),
            pltpu.VMEM((2, HEAD_N, BLOCK_LEN, 128), f32),
            pltpu.VMEM((PAIRS, BLOCK_LEN, 128), f32),
            pltpu.VMEM((PAIRS, BLOCK_LEN, 128), f32),
            pltpu.VMEM((2,) + square, f32),
            pltpu.VMEM(square, f32),
            pltpu.VMEM(square, bf16),
            pltpu.VMEM((PAIRS, 128, state), bf16),
            pltpu.VMEM((BLOCK_LEN, state), f32),
            dma((MDL,)), dma((MDL,)), dma((MDL,)), dma((MDL,)),
            dma((2, MDL)), dma((2, MDL)), dma((2, MDL)), dma((2, MDL)),
            dma, dma, dma((2,)), dma((2,)),
        ],
        compiler_params=pltpu.CompilerParams(
            collective_id=0, has_side_effects=True, vmem_limit_bytes=56 * 1024 * 1024
        ),
    )(
        layer_input.reshape(length, cols).T, read_weight, head_inputs, write_vectors,
        jnp.transpose(log_decay, (1, 0, 2)), segment_ids, out_grad,
    )


def fits(mesh, values):
    (layer_input, _, head_inputs, write_vectors, log_decay, _, _) = values
    return (
        mesh.shape["ctx"] == 1
        and mesh.shape["mdl"] == MDL
        and mesh.shape["dp"] == 2
        and layer_input.shape[:2] == (1, 2 * BLOCK_LEN)
        and log_decay.shape[1] == HEAD_N
        and head_inputs.shape[2] == HEAD_N * 64
        and write_vectors.shape[2] == 128
    )


def solution(mesh):
    def chosen(*values):
        if fits(mesh, values):
            return fused(*values)
        return per_device(*values)

    placed = (
        P(("grp", "dp"), "ctx", "mdl"),
        P("mdl", None),
        P(("grp", "dp"), "ctx", "mdl"),
        P(("grp", "dp"), "ctx", None),
        P(("grp", "dp"), "mdl", "ctx"),
        P(("grp", "dp"), "ctx"),
        P(("grp", "dp"), "ctx", "mdl"),
    )
    return jax.shard_map(
        chosen,
        mesh=mesh,
        in_specs=placed,
        out_specs=(P(("grp", "dp"), "ctx", "mdl"), P(("grp", "ctx", "dp"), "mdl")),
        check_vma=False,
    )
```

```python
import jax
import jax.numpy as jnp
from jax import lax
from jax.experimental import pallas as pl
from jax.experimental.pallas import tpu as pltpu
from jax.sharding import PartitionSpec as P

BLOCK_LEN = 512
MESH = pl.DeviceIdType.MESH
MDL = 8
SHARE = 2 * BLOCK_LEN // MDL
HALF = BLOCK_LEN // MDL
HEAD_N = 10
PAIRS = HEAD_N // 2
TILE = 256
FAR_FIRST = (4, 5, 3, 6, 2, 7, 1)
LOG2E = 1.4426950408889634


def shifted(value, axis, by):
    count = lax.axis_size(axis)
    pairs = [(i, i + by) for i in range(count) if 0 <= i + by < count]
    return lax.ppermute(value, axis, pairs)


def join_parts(earlier, later):
    early_first, early_last, early_pass, leading_state = earlier
    later_first, later_last, later_pass, later_state = later
    linked = jnp.logical_or(
        early_last == later_first, jnp.logical_or(early_last < 0.0, later_first < 0.0)
    )
    carried = later_pass * linked.astype(jnp.float32)[..., None]
    front_seg = jnp.where(early_first < 0.0, later_first, early_first)
    back_seg = jnp.where(later_last < 0.0, early_last, later_last)
    return (
        front_seg,
        back_seg,
        early_pass * carried,
        later_state + carried[..., None, None] * leading_state,
    )


def per_device(
    layer_input, read_weight, head_inputs, write_vectors, log_decay, segment_ids, out_grad
):
    trace_count, length, model_cols = layer_input.shape
    head_count = log_decay.shape[1]
    head_dim = head_inputs.shape[2] // head_count
    state_dim = write_vectors.shape[2]
    block_count = length // BLOCK_LEN
    rows_all = trace_count * length
    flat_count = trace_count * block_count
    flat_input = layer_input.reshape(rows_all, model_cols)
    partial_value = jnp.dot(flat_input, read_weight, preferred_element_type=jnp.float32)
    readout = lax.psum(partial_value.astype(jnp.bfloat16), "mdl")
    segments = segment_ids.astype(jnp.float32).reshape(trace_count, block_count, BLOCK_LEN)
    decays = log_decay.reshape(trace_count, head_count, block_count, BLOCK_LEN)
    positions = jnp.arange(BLOCK_LEN)
    upper = (positions[:, None] <= positions[None, :]).astype(jnp.float32)
    cumulative = jnp.einsum("bhks,st->bhkt", decays, upper, precision=lax.Precision.HIGHEST)
    closing = cumulative[..., -1:]
    at_end = (segments == segments[..., -1:]).astype(jnp.float32)
    end_weight = jnp.exp(closing - cumulative) * at_end[:, None]
    values = head_inputs.reshape(trace_count, block_count, BLOCK_LEN, head_count, head_dim)
    keys_block = write_vectors.reshape(trace_count, block_count, BLOCK_LEN, state_dim)
    weighted = (values * jnp.transpose(end_weight, (0, 2, 3, 1))[..., None]).astype(jnp.bfloat16)
    block_states = jnp.einsum(
        "bkqhp,bkqn->kbhpn", weighted, keys_block, preferred_element_type=jnp.float32
    )
    front_seg = jnp.transpose(segments[..., 0])
    back_seg = jnp.transpose(segments[..., -1])
    single = (front_seg == back_seg).astype(jnp.float32)
    through = jnp.exp(jnp.transpose(closing[..., 0], (2, 0, 1))) * single[..., None]
    neutral = (
        -jnp.ones((trace_count,), jnp.float32),
        -jnp.ones((trace_count,), jnp.float32),
        jnp.ones((trace_count, head_count), jnp.float32),
        jnp.zeros((trace_count, head_count, head_dim, state_dim), jnp.float32),
    )

    def absorb(running, pieces):
        return (join_parts(running, pieces), running)

    device_total, prefixes = lax.scan(absorb, neutral, (front_seg, back_seg, through, block_states))
    position = lax.axis_index("ctx")

    def relay_once(iteration, incoming):
        outgoing = join_parts(incoming, device_total)
        shifted_lines = shifted((outgoing[0], outgoing[1], outgoing[2], outgoing[3]), "ctx", 1)
        return tuple(
            (
                jnp.where(position == 0, anchor, arrived)
                for anchor, arrived in zip(neutral, shifted_lines)
            )
        )

    entering = lax.fori_loop(0, lax.axis_size("ctx") - 1, relay_once, neutral)
    starts = join_parts(entering, prefixes)
    start_low = starts[3].astype(jnp.bfloat16)
    prior_seg = jnp.transpose(starts[1])
    coupled_items = (segments == prior_seg[..., None]).astype(jnp.float32)
    entry_gain = jnp.exp(cumulative) * coupled_items[:, None]
    gain_rows = jnp.transpose(entry_gain, (0, 2, 3, 1))[..., None]
    readout_block = readout.reshape(trace_count, block_count, BLOCK_LEN, state_dim)
    grads_block = out_grad.reshape(trace_count, block_count, BLOCK_LEN, head_count, head_dim)
    carried_out = (
        jnp.einsum(
            "bkqn,kbhpn->bkqhp", readout_block, start_low, preferred_element_type=jnp.float32
        )
        * gain_rows
    )
    per_head = jnp.einsum(
        "bkqhp,kbhpn->bkqhn", grads_block, start_low, preferred_element_type=jnp.float32
    )
    carried_back = jnp.sum(per_head * gain_rows, axis=3)
    causal = positions[:, None] >= positions[None, :]

    def inside(pieces):
        read_rows, key_rows, value_rows, grad_rows, cum_rows, seg_rows = pieces
        allowed = jnp.logical_and(causal, seg_rows[:, None] == seg_rows[None, :])
        spread = cum_rows[:, :, None] - cum_rows[:, None, :]
        weight = jnp.where(allowed[None], jnp.exp(jnp.where(allowed[None], spread, 0.0)), 0.0)
        scores = jnp.einsum("tn,sn->ts", read_rows, key_rows, preferred_element_type=jnp.float32)
        blend_factor = (weight * scores[None]).astype(jnp.bfloat16)
        inside_out = jnp.einsum(
            "hts,shp->thp", blend_factor, value_rows, preferred_element_type=jnp.float32
        )
        products = jnp.einsum(
            "thp,shp->hts", grad_rows, value_rows, preferred_element_type=jnp.float32
        )
        response = jnp.sum(weight * products, axis=0).astype(jnp.bfloat16)
        inside_back = jnp.dot(response, key_rows, preferred_element_type=jnp.float32)
        return (inside_out, inside_back)

    own_out, own_back = lax.map(
        inside,
        (
            readout_block.reshape(flat_count, BLOCK_LEN, state_dim),
            keys_block.reshape(flat_count, BLOCK_LEN, state_dim),
            values.reshape(flat_count, BLOCK_LEN, head_count, head_dim),
            grads_block.reshape(flat_count, BLOCK_LEN, head_count, head_dim),
            jnp.transpose(cumulative, (0, 2, 1, 3)).reshape(flat_count, head_count, BLOCK_LEN),
            segments.reshape(flat_count, BLOCK_LEN),
        ),
    )
    total_out = (
        own_out.reshape(trace_count, block_count, BLOCK_LEN, head_count, head_dim) + carried_out
    )
    head_outputs = total_out.astype(jnp.bfloat16).reshape(
        trace_count, length, head_count * head_dim
    )
    back_part = (
        own_back.reshape(trace_count, block_count, BLOCK_LEN, state_dim) + carried_back
    ).reshape(rows_all, state_dim)
    read_back = lax.psum(back_part.astype(jnp.bfloat16), "mdl")
    read_grad = lax.psum_scatter(
        lax.dot_general(
            read_back, flat_input, (((0,), (0,)), ((), ())), preferred_element_type=jnp.float32
        ),
        ("ctx", "dp"),
        scatter_dimension=0,
        tiled=True,
    )
    return (head_outputs, read_grad)


def fused_kernel(
    x_ref, w_ref, hi_hbm, wv_ref, ld_ref, seg_ref, og_hbm, out_hbm, grad_ref,
    hi_ref, og_ref, out_ref, kept,
    part, rs1, readout, back, rs2, rb, gfull, grecv,
    split, stack, rowx, colx, endx, entx, bias, resp, scores, start, carry,
    rs1_s, rs1_r, ag1_s, ag1_r, rs2_s, rs2_r, ag2_s, ag2_r, dp_s, dp_r, in_s, out_s,
):
    f32, bf16 = jnp.float32, jnp.bfloat16
    load_hi = pltpu.make_async_copy(hi_hbm, hi_ref, in_s.at[0])
    load_og = pltpu.make_async_copy(og_hbm, og_ref, in_s.at[1])
    load_hi.start()
    load_og.start()
    me = lax.axis_index("mdl")
    core = lax.axis_index("dp")
    peers = [lax.rem(me + o, MDL) for o in range(MDL)]
    barrier = pltpu.get_barrier_semaphore()
    for o in range(1, MDL):
        pl.semaphore_signal(barrier, inc=1, device_id={"mdl": peers[o]}, device_id_type=MESH)
    pl.semaphore_signal(barrier, inc=1, device_id={"dp": 1 - core}, device_id_type=MESH)

    def remote(src, dst, send, recv, to):
        copy = pltpu.make_async_remote_copy(
            src_ref=src, dst_ref=dst, send_sem=send, recv_sem=recv,
            device_id=to, device_id_type=MESH,
        )
        copy.start()
        return copy

    nn = (((1,), (1,)), ((), ()))
    tt = (((0,), (0,)), ((), ()))
    part[...] = lax.dot_general(x_ref[...], w_ref[...], tt, preferred_element_type=f32).astype(bf16)
    pl.semaphore_wait(barrier, MDL)
    first = [
        remote(
            part.at[pl.ds(pl.multiple_of(peers[o] * SHARE, SHARE), SHARE)], rs1.at[o],
            rs1_s.at[o], rs1_r.at[o], {"mdl": peers[o]},
        )
        for o in FAR_FIRST
    ]

    lane = lax.broadcasted_iota(jnp.int32, (1, 128), 1)
    left = lane < 64
    mask_a = left.astype(f32).astype(bf16)
    mask_b = (1.0 - left.astype(f32)).astype(bf16)
    rows_i = lax.broadcasted_iota(jnp.int32, (BLOCK_LEN, BLOCK_LEN), 0)
    cols_i = lax.broadcasted_iota(jnp.int32, (BLOCK_LEN, BLOCK_LEN), 1)
    upper = (rows_i <= cols_i).astype(f32).astype(bf16)

    def prepare(k):
        span = pl.ds(k * BLOCK_LEN, BLOCK_LEN)
        split[...] = jnp.zeros_like(split)
        stack[...] = jnp.zeros_like(stack)
        for h in range(HEAD_N):
            stack[pl.ds(h, 1), :] = ld_ref[h, :, span]
        rest = stack[pl.ds(0, 16), :]
        for piece in range(3):
            high = rest.astype(bf16).astype(f32)
            split[pl.ds(16 * piece, 16), :] = high
            rest = rest - high
        sums = jnp.dot(split[...].astype(bf16), upper, preferred_element_type=f32)
        cum = (sums[0:16] + sums[16:32] + sums[32:48]) * LOG2E
        seg = seg_ref[:, span].astype(f32)
        stack[pl.ds(0, 16), :] = cum
        if k == 0:
            close = cum[:, BLOCK_LEN - 1 :]
            at_end = (seg == seg[:, BLOCK_LEN - 1 :]).astype(f32)
            stack[pl.ds(16, 16), :] = jnp.exp2(close - cum) * at_end
        else:
            prior = seg_ref[:, pl.ds(BLOCK_LEN - 128, 128)].astype(f32)[:, 127:]
            stack[pl.ds(32, 16), :] = jnp.exp2(cum) * (seg == prior).astype(f32)
        stack[pl.ds(48, 8), :] = jnp.broadcast_to(seg, (8, BLOCK_LEN))
        turned = stack[...].T
        for h in range(HEAD_N):
            rowx[k, h] = cum[h : h + 1, :]
            colx[k, h] = jnp.broadcast_to(turned[:, h : h + 1], (BLOCK_LEN, 128))
        for j in range(PAIRS):
            base, target = (16, endx) if k == 0 else (32, entx)
            a = turned[:, base + 2 * j : base + 2 * j + 1]
            b = turned[:, base + 2 * j + 1 : base + 2 * j + 2]
            target[j] = jnp.where(left, a, b)
        same = jnp.logical_and(turned[:, 48:49] == seg, rows_i >= cols_i)
        bias[k] = jnp.where(same, 0.0, -1e30)

    def weight(k, h, i, wide):
        rows = pl.ds(i * TILE, TILE)
        col = colx[k, h, rows, :]
        col = jnp.concatenate([col] * (wide // 128), axis=1)
        return jnp.exp2((col - rowx[k, h, :, pl.ds(0, wide)]) + bias[k, rows, pl.ds(0, wide)])

    def lanes_of(j):
        return pl.ds(pl.multiple_of(j * 128, 128), 128)

    def backward(k):
        resp[...] = jnp.zeros_like(resp)
        carry[...] = jnp.zeros_like(carry)
        keys = wv_ref[0, pl.ds(k * BLOCK_LEN, BLOCK_LEN), :]

        def body(j, _):
            lanes = lanes_of(j)
            if k == 0:
                value = hi_ref[0, pl.ds(0, BLOCK_LEN), lanes].astype(f32)
                low = (value * endx[j]).astype(bf16)
                start[j] = lax.dot_general(low, keys, tt, preferred_element_type=f32).astype(bf16)
            else:
                grads = og_ref[0, pl.ds(BLOCK_LEN, BLOCK_LEN), lanes].astype(f32)
                carry[...] += jnp.dot(
                    (grads * entx[j]).astype(bf16), start[j], preferred_element_type=f32
                )
            for i in range(BLOCK_LEN // TILE):
                wide = (i + 1) * TILE
                value = hi_ref[0, pl.ds(k * BLOCK_LEN, wide), lanes]
                grads = og_ref[0, pl.ds(k * BLOCK_LEN + i * TILE, TILE), lanes]
                pa = lax.dot_general(grads * mask_a, value, nn, preferred_element_type=f32)
                pb = lax.dot_general(grads * mask_b, value, nn, preferred_element_type=f32)
                wa = weight(k, 2 * j, i, wide)
                wb = weight(k, 2 * j + 1, i, wide)
                rows = pl.ds(i * TILE, TILE)
                kept[k, 2 * j, rows, pl.ds(0, wide)] = wa.astype(bf16)
                kept[k, 2 * j + 1, rows, pl.ds(0, wide)] = wb.astype(bf16)
                resp[rows, pl.ds(0, wide)] += wa * pa + wb * pb
            return 0

        lax.fori_loop(0, PAIRS, body, 0)
        total = jnp.dot(resp[...].astype(bf16), keys, preferred_element_type=f32) + carry[...]
        back[pl.ds(k * BLOCK_LEN, BLOCK_LEN), :] = total.astype(bf16)
        return [
            remote(
                back.at[pl.ds(pl.multiple_of(k * BLOCK_LEN + peers[o] * HALF, HALF), HALF)],
                rs2.at[k, o], rs2_s.at[k, o], rs2_r.at[k, o], {"mdl": peers[o]},
            )
            for o in FAR_FIRST
        ]

    def forward(k):
        keys = wv_ref[0, pl.ds(k * BLOCK_LEN, BLOCK_LEN), :]
        reads = readout[pl.ds(k * BLOCK_LEN, BLOCK_LEN), :]
        scores[...] = lax.dot_general(reads, keys, nn, preferred_element_type=f32).astype(bf16)

        def body(j, _):
            lanes = lanes_of(j)
            for i in range(BLOCK_LEN // TILE):
                wide = (i + 1) * TILE
                value = hi_ref[0, pl.ds(k * BLOCK_LEN, wide), lanes]
                rows = pl.ds(i * TILE, TILE)
                score = scores[rows, pl.ds(0, wide)]
                mix_a = kept[k, 2 * j, rows, pl.ds(0, wide)] * score
                mix_b = kept[k, 2 * j + 1, rows, pl.ds(0, wide)] * score
                oa = jnp.dot(mix_a, value, preferred_element_type=f32)
                ob = jnp.dot(mix_b, value, preferred_element_type=f32)
                total = jnp.where(left, oa, ob)
                if k == 1:
                    carried = lax.dot_general(
                        readout[pl.ds(BLOCK_LEN + i * TILE, TILE), :], start[j], nn,
                        preferred_element_type=f32,
                    )
                    total = total + carried * entx[j, pl.ds(i * TILE, TILE), :]
                out_ref[0, pl.ds(k * BLOCK_LEN + i * TILE, TILE), lanes] = total.astype(bf16)
            return 0

        lax.fori_loop(0, PAIRS, body, 0)
        span = pl.ds(k * BLOCK_LEN, BLOCK_LEN)
        store = pltpu.make_async_copy(out_ref.at[:, span], out_hbm.at[:, span], out_s.at[k])
        store.start()
        return store

    across = me + 1 - 2 * lax.rem(me, 2)
    lines = [lax.rem(me + 2 * q, MDL) for q in range(4)]
    origins = [lax.rem(me + MDL - 2 * q, MDL) for q in range(4)]

    def gather(ref, begin, size, send, recv):
        mine = pl.ds(pl.multiple_of(begin + me * size, size), size)
        near = [
            remote(ref.at[mine], ref.at[mine], send(q), recv(q), {"mdl": lines[q]})
            for q in (2, 3, 1)
        ]
        return near, [remote(ref.at[mine], ref.at[mine], send(4), recv(4), {"mdl": across})]

    def relay(copies, ref, begin, size, send, recv):
        near, far = copies
        for at in (2, 1, 0):
            q = (2, 3, 1)[at]
            near[at].wait_recv()
            rows = pl.ds(pl.multiple_of(begin + origins[q] * size, size), size)
            far.append(
                remote(ref.at[rows], ref.at[rows], send(4 + q), recv(4 + q), {"mdl": across})
            )
        return near + far, far

    sems_1 = (lambda o: ag1_s.at[o]), (lambda o: ag1_r.at[o])
    sems_2 = [
        ((lambda o: ag2_s.at[0, o]), (lambda o: ag2_r.at[0, o])),
    ]

    def collect(k, copies):
        mine = pl.ds(pl.multiple_of(k * BLOCK_LEN + me * HALF, HALF), HALF)
        total = back[mine, :].astype(f32)
        for o in range(1, MDL):
            copies[FAR_FIRST.index(o)].wait_recv()
            total = total + rs2[k, o].astype(f32)
        rb[mine, :] = total.astype(bf16)
        if k == 0:
            return gather(rb, 0, HALF, *sems_2[0])
        return [
            remote(rb.at[mine], rb.at[mine], ag2_s.at[1, o], ag2_r.at[1, o], {"mdl": peers[o]})
            for o in FAR_FIRST
        ]

    prepare(0)
    load_hi.wait()
    load_og.wait()
    back_0 = backward(0)
    mine = pl.ds(pl.multiple_of(me * SHARE, SHARE), SHARE)
    total = part[mine, :].astype(f32)
    for o in range(1, MDL):
        first[FAR_FIRST.index(o)].wait_recv()
        total = total + rs1[o].astype(f32)
    readout[mine, :] = total.astype(bf16)
    spread = gather(readout, 0, SHARE, *sems_1)
    prepare(1)
    back_1 = backward(1)
    spread, landing = relay(spread, readout, 0, SHARE, *sems_1)
    gather_0 = collect(0, back_0)
    for copy in landing:
        copy.wait_recv()
    store_0 = forward(0)
    gather_1 = collect(1, back_1)
    gather_0, landing_0 = relay(gather_0, rb, 0, HALF, *sems_2[0])
    store_1 = forward(1)
    for copy in landing_0:
        copy.wait_recv()
    turn = (((0,), (1,)), ((), ()))
    halves = [pl.ds(0, BLOCK_LEN), pl.ds(BLOCK_LEN, BLOCK_LEN)]
    gfull[...] = lax.dot_general(
        rb[halves[0], :], x_ref[:, halves[0]], turn, preferred_element_type=f32
    )
    for copy in gather_1:
        copy.wait_recv()
    gfull[...] += lax.dot_general(
        rb[halves[1], :], x_ref[:, halves[1]], turn, preferred_element_type=f32
    )
    owner = 1 - core
    swap = remote(
        gfull.at[pl.ds(pl.multiple_of(owner * 64, 64), 64)], grecv, dp_s, dp_r, {"dp": owner}
    )
    swap.wait_recv()
    grad_ref[...] = gfull[pl.ds(pl.multiple_of(core * 64, 64), 64), :] + grecv[...]
    swap.wait_send()
    store_0.wait()
    store_1.wait()
    for copy in first + spread + back_0 + back_1 + gather_0 + gather_1:
        copy.wait_send()


def fused(layer_input, read_weight, head_inputs, write_vectors, log_decay, segment_ids, out_grad):
    f32, bf16 = jnp.float32, jnp.bfloat16
    dma = pltpu.SemaphoreType.DMA
    vmem = pl.BlockSpec(memory_space=pltpu.VMEM)
    anywhere = pl.BlockSpec(memory_space=pl.ANY)
    length = layer_input.shape[1]
    cols = layer_input.shape[2]
    state = write_vectors.shape[2]
    square = (BLOCK_LEN, BLOCK_LEN)
    return pl.pallas_call(
        fused_kernel,
        out_shape=(
            jax.ShapeDtypeStruct(head_inputs.shape, bf16),
            jax.ShapeDtypeStruct((state // 2, cols), f32),
        ),
        in_specs=[vmem, vmem, anywhere, vmem, vmem, vmem, anywhere],
        out_specs=(anywhere, vmem),
        scratch_shapes=[
            pltpu.VMEM(head_inputs.shape, bf16),
            pltpu.VMEM(head_inputs.shape, bf16),
            pltpu.VMEM(head_inputs.shape, bf16),
            pltpu.VMEM((2, HEAD_N) + square, bf16),
            pltpu.VMEM((length, state), bf16),
            pltpu.VMEM((MDL, SHARE, state), bf16),
            pltpu.VMEM((length, state), bf16),
            pltpu.VMEM((length, state), bf16),
            pltpu.VMEM((2, MDL, HALF, state), bf16),
            pltpu.VMEM((length, state), bf16),
            pltpu.VMEM((state, cols), f32),
            pltpu.VMEM((state // 2, cols), f32),
            pltpu.VMEM((48, BLOCK_LEN), f32),
            pltpu.VMEM((128, BLOCK_LEN), f32),
            pltpu.VMEM((2, HEAD_N, 1, BLOCK_LEN), f32),
            pltpu.VMEM((2, HEAD_N, BLOCK_LEN, 128), f32),
            pltpu.VMEM((PAIRS, BLOCK_LEN, 128), f32),
            pltpu.VMEM((PAIRS, BLOCK_LEN, 128), f32),
            pltpu.VMEM((2,) + square, f32),
            pltpu.VMEM(square, f32),
            pltpu.VMEM(square, bf16),
            pltpu.VMEM((PAIRS, 128, state), bf16),
            pltpu.VMEM((BLOCK_LEN, state), f32),
            dma((MDL,)), dma((MDL,)), dma((MDL,)), dma((MDL,)),
            dma((2, MDL)), dma((2, MDL)), dma((2, MDL)), dma((2, MDL)),
            dma, dma, dma((2,)), dma((2,)),
        ],
        compiler_params=pltpu.CompilerParams(
            collective_id=0, has_side_effects=True, vmem_limit_bytes=56 * 1024 * 1024
        ),
    )(
        layer_input.reshape(length, cols).T, read_weight, head_inputs, write_vectors,
        jnp.transpose(log_decay, (1, 0, 2)), segment_ids, out_grad,
    )


def fits(mesh, values):
    (layer_input, _, head_inputs, write_vectors, log_decay, _, _) = values
    return (
        mesh.shape["ctx"] == 1
        and mesh.shape["mdl"] == MDL
        and mesh.shape["dp"] == 2
        and layer_input.shape[:2] == (1, 2 * BLOCK_LEN)
        and log_decay.shape[1] == HEAD_N
        and head_inputs.shape[2] == HEAD_N * 64
        and write_vectors.shape[2] == 128
    )


def solution(mesh):
    def chosen(*values):
        if fits(mesh, values):
            return fused(*values)
        return per_device(*values)

    placed = (
        P(("grp", "dp"), "ctx", "mdl"),
        P("mdl", None),
        P(("grp", "dp"), "ctx", "mdl"),
        P(("grp", "dp"), "ctx", None),
        P(("grp", "dp"), "mdl", "ctx"),
        P(("grp", "dp"), "ctx"),
        P(("grp", "dp"), "ctx", "mdl"),
    )
    return jax.shard_map(
        chosen,
        mesh=mesh,
        in_specs=placed,
        out_specs=(P(("grp", "dp"), "ctx", "mdl"), P(("grp", "ctx", "dp"), "mdl")),
        check_vma=False,
    )
```
